32 devices in a mesh: az: 8 (over z, x), rad: 4 (over y, core).
Axes of the slice: x: 2, y: 2, z: 4, core: 2. Of those that a mesh axis runs over, the one named last changes fastest.
Arguments:
- fields: float32 [8, 64, 256, 128], P(None, 'rad', 'az'), as said below
- offsets: int32 [64], replicated, may hold values from 0 to 255
- boundary_shift: int32 [1], replicated, may hold values from 0 to 255
Outputs:
- advanced: float32 [8, 64, 256, 128], P(None, 'rad', 'az')
The draws below stay inside these ranges and needn't reach their ends.
Inputs may be any that keep to these rules, and one draw needn't show every extreme that they name: Each cell of fields is a conserved state whose density and implied pressure lie between 0.5 and 2; velocities stay under 1.8 and field components under 0.9 in magnitude.
All inputs are finite; a program needn't handle non-finite values.
Results may differ from the reference program's by a relative error of at most 0.0003.
Values sent between devices are 32-bit elements; how exact they have to be, the bound alone decides.
A program may use at most 192 MiB of HBM per device.

```python
import jax
import jax.numpy as jnp
from jax import lax

CX = 16
NX = 64
NY = 256
NZ = 128
N_RAD = 4


GAMMA_RATIO = 5.0 / 3.0


def draw_fields(key, part):
    subkeys = jax.random.split(key, 4)
    grid_shape = (NX, NY, NZ)
    radial_ramp = 1.0 + 2.0 * jnp.arange(NX, dtype=jnp.float32)[:, None, None] / max(NX - 1, 1)
    density = jnp.exp(jax.random.uniform(subkeys[0], grid_shape, jnp.float32, -0.69, 0.69))
    pressure = jnp.exp(jax.random.uniform(subkeys[1], grid_shape, jnp.float32, -0.69, 0.69))
    velocity = jnp.clip(0.2 * jax.random.normal(subkeys[2], (3,) + grid_shape, jnp.float32), -0.6, 0.6) * radial_ramp
    magnetic = jnp.clip(0.3 * jax.random.normal(subkeys[3], (3,) + grid_shape, jnp.float32), -0.9, 0.9)
    momentum = density * velocity
    energy = pressure / (GAMMA_RATIO - 1.0) + 0.5 * density * jnp.sum(velocity * velocity, axis=0) + 0.5 * jnp.sum(magnetic * magnetic, axis=0)
    return jnp.concatenate([density[None], momentum, energy[None], magnetic], axis=0).astype(jnp.float32)


def with_ends(array, key, smallest, high):
    longest = array.shape.index(max(array.shape))
    spots = []
    for shift in (0, 1):
        where = [jax.random.randint(jax.random.fold_in(key, axis), (), 0, length) for axis, length in enumerate(array.shape)]
        where[longest] = (where[longest] + shift) % array.shape[longest]
        spots.append(tuple(where))
    return array.at[spots[0]].set(smallest).at[spots[1]].set(high)


def setup_inputs(seed: int = 0) -> dict:
    key_of = jax.random.split(jax.random.key(seed), 4)
    return {
        "fields": draw_fields(jax.random.fold_in(key_of[3], 71), 0),
        "offsets": with_ends(jax.random.randint(key_of[1], (NX,), 0, NY), jax.random.fold_in(key_of[1], 1), 0, NY - 1).astype(jnp.int32),
        "boundary_shift": jax.random.randint(key_of[2], (1,), 0, NY).astype(jnp.int32),
    }


GAMMA_RATIO = 5.0 / 3.0
CFL_NUMBER = 0.4
OMEGA_RATE = 1.0
SHEAR_RATE = 1.5

def primitive(state):
    density = state[0]
    inverse = 1.0 / density
    speed_x = state[1] * inverse
    speed_y = state[2] * inverse
    speed_z = state[3] * inverse
    kinetic = 0.5 * density * (speed_x * speed_x + speed_y * speed_y + speed_z * speed_z)
    magnetic = 0.5 * (state[5] * state[5] + state[6] * state[6] + state[7] * state[7])
    pressure = (GAMMA_RATIO - 1.0) * (state[4] - kinetic - magnetic)
    return (density, speed_x, speed_y, speed_z, pressure, state[5], state[6], state[7])

def fast_speed(density, pressure, normal_field, field_sq):
    sound = (GAMMA_RATIO * pressure + field_sq) / density
    spread = jnp.maximum(sound * sound - 4.0 * GAMMA_RATIO * pressure * normal_field * normal_field / (density * density), 0.0)
    return jnp.sqrt(0.5 * (sound + jnp.sqrt(spread)))

def cell_speed(primitives):
    field_sq = primitives[5] * primitives[5] + primitives[6] * primitives[6] + primitives[7] * primitives[7]
    total = jnp.abs(primitives[1]) + fast_speed(primitives[0], primitives[4], primitives[5], field_sq)
    total = total + jnp.abs(primitives[2]) + fast_speed(primitives[0], primitives[4], primitives[6], field_sq)
    total = total + jnp.abs(primitives[3]) + fast_speed(primitives[0], primitives[4], primitives[7], field_sq)
    return total

def minmod(first_diff, second_diff):
    return 0.5 * (jnp.sign(first_diff) + jnp.sign(second_diff)) * jnp.minimum(jnp.abs(first_diff), jnp.abs(second_diff))

def take_range(values, start_at, stop_at, along):
    return lax.slice_in_dim(values, start_at, stop_at, axis=along)

def side_terms(values, normal_field):
    density, normal_speed, trans_speed, other_speed, pressure = (values[0], values[1], values[2], values[3], values[4])
    trans_field, other_field = (values[6], values[7])
    field_sq = normal_field * normal_field + trans_field * trans_field + other_field * other_field
    total_press = pressure + 0.5 * field_sq
    energy = pressure / (GAMMA_RATIO - 1.0) + 0.5 * density * (normal_speed * normal_speed + trans_speed * trans_speed + other_speed * other_speed) + 0.5 * field_sq
    field_work = normal_speed * normal_field + trans_speed * trans_field + other_speed * other_field
    conserved = (density, density * normal_speed, density * trans_speed, density * other_speed, energy, normal_field, trans_field, other_field)
    fluxes = (density * normal_speed, density * normal_speed * normal_speed + total_press - normal_field * normal_field, density * normal_speed * trans_speed - normal_field * trans_field, density * normal_speed * other_speed - normal_field * other_field, (energy + total_press) * normal_speed - normal_field * field_work, jnp.zeros_like(density), trans_field * normal_speed - normal_field * trans_speed, other_field * normal_speed - normal_field * other_speed)
    signal = fast_speed(density, pressure, normal_field, field_sq)
    return (conserved, fluxes, total_press, energy, field_work, signal)

def star_state(values, energy, total_press, field_work, normal_field, outer, middle, star_press):
    density, normal_speed, trans_speed, other_speed = (values[0], values[1], values[2], values[3])
    trans_field, other_field = (values[6], values[7])
    relative = outer - normal_speed
    distance = outer - middle
    star_density = density * relative / distance
    product = density * relative * distance
    divisor = jnp.maximum(product - normal_field * normal_field, 0.5 * product)
    trans_star = trans_speed - normal_field * trans_field * (middle - normal_speed) / divisor
    other_star = other_speed - normal_field * other_field * (middle - normal_speed) / divisor
    factor = (density * relative * relative - normal_field * normal_field) / divisor
    trans_bstar = trans_field * factor
    other_bstar = other_field * factor
    star_work = middle * normal_field + trans_star * trans_bstar + other_star * other_bstar
    star_energy = (relative * energy - total_press * normal_speed + star_press * middle + normal_field * (field_work - star_work)) / distance
    return (star_density, trans_star, other_star, trans_bstar, other_bstar, star_work, star_energy)

def hlld_flux(left_values, right_values):
    normal_field = 0.5 * (left_values[5] + right_values[5])
    cons_left, flux_left, press_left, energy_left, work_left, signal_left = side_terms(left_values, normal_field)
    cons_right, flux_right, press_right, energy_right, work_right, signal_right = side_terms(right_values, normal_field)
    fastest = jnp.maximum(signal_left, signal_right)
    lower = jnp.minimum(left_values[1], right_values[1]) - fastest
    upper = jnp.maximum(left_values[1], right_values[1]) + fastest
    mass_left = left_values[0] * (lower - left_values[1])
    mass_right = right_values[0] * (upper - right_values[1])
    guess = (mass_right * right_values[1] - mass_left * left_values[1] - press_right + press_left) / (mass_right - mass_left)
    margin = 0.1 * (upper - lower)
    middle = jnp.clip(guess, lower + margin, upper - margin)
    star_press = press_left + mass_left * (middle - left_values[1])
    dens_left, trans_left, other_left, tfield_left, ofield_left, swork_left, senergy_left = star_state(left_values, energy_left, press_left, work_left, normal_field, lower, middle, star_press)
    dens_right, trans_right, other_right, tfield_right, ofield_right, swork_right, senergy_right = star_state(right_values, energy_right, press_right, work_right, normal_field, upper, middle, star_press)
    root_left = jnp.sqrt(dens_left)
    root_right = jnp.sqrt(dens_right)
    sign_field = jnp.sign(normal_field)
    root_sum = root_left + root_right
    trans_double = (root_left * trans_left + root_right * trans_right + (tfield_right - tfield_left) * sign_field) / root_sum
    other_double = (root_left * other_left + root_right * other_right + (ofield_right - ofield_left) * sign_field) / root_sum
    tfield_double = (root_left * tfield_right + root_right * tfield_left + root_left * root_right * (trans_right - trans_left) * sign_field) / root_sum
    ofield_double = (root_left * ofield_right + root_right * ofield_left + root_left * root_right * (other_right - other_left) * sign_field) / root_sum
    double_work = middle * normal_field + trans_double * tfield_double + other_double * ofield_double
    denergy_left = senergy_left - root_left * (swork_left - double_work) * sign_field
    denergy_right = senergy_right + root_right * (swork_right - double_work) * sign_field
    inner_left = middle - jnp.abs(normal_field) / root_left
    inner_right = middle + jnp.abs(normal_field) / root_right
    star_cons_left = (dens_left, dens_left * middle, dens_left * trans_left, dens_left * other_left, senergy_left, normal_field, tfield_left, ofield_left)
    star_cons_right = (dens_right, dens_right * middle, dens_right * trans_right, dens_right * other_right, senergy_right, normal_field, tfield_right, ofield_right)
    double_cons_left = (dens_left, dens_left * middle, dens_left * trans_double, dens_left * other_double, denergy_left, normal_field, tfield_double, ofield_double)
    double_cons_right = (dens_right, dens_right * middle, dens_right * trans_double, dens_right * other_double, denergy_right, normal_field, tfield_double, ofield_double)
    outcome = []
    for component in range(8):
        star_left = flux_left[component] + lower * (star_cons_left[component] - cons_left[component])
        double_left = star_left + inner_left * (double_cons_left[component] - star_cons_left[component])
        star_right = flux_right[component] + upper * (star_cons_right[component] - cons_right[component])
        double_right = star_right + inner_right * (double_cons_right[component] - star_cons_right[component])
        chosen = jnp.where(lower > 0, flux_left[component], jnp.where(inner_left > 0, star_left, jnp.where(middle > 0, double_left, jnp.where(inner_right > 0, double_right, jnp.where(upper > 0, star_right, flux_right[component])))))
        outcome.append(chosen)
    outcome[5] = jnp.zeros_like(outcome[0])
    return outcome

def direction_divergence(primitives, along, normal_order):
    mapping = (0, normal_order[0], normal_order[1], normal_order[2], 4, normal_order[0] + 4, normal_order[1] + 4, normal_order[2] + 4)
    left_faces = []
    right_faces = []
    for component in range(8):
        values = primitives[mapping[component]]
        length = values.shape[along]
        cell_count = length - 4
        differences = take_range(values, 1, length, along) - take_range(values, 0, length - 1, along)
        slopes = minmod(take_range(differences, 0, length - 2, along), take_range(differences, 1, length - 1, along))
        centres = take_range(values, 1, length - 1, along)
        left_faces.append(take_range(centres, 0, cell_count + 1, along) + 0.5 * take_range(slopes, 0, cell_count + 1, along))
        right_faces.append(take_range(centres, 1, cell_count + 2, along) - 0.5 * take_range(slopes, 1, cell_count + 2, along))
    face_fluxes = hlld_flux(left_faces, right_faces)
    result = [None] * 8
    for component in range(8):
        face_values = face_fluxes[component]
        length = face_values.shape[along]
        result[mapping[component]] = take_range(face_values, 1, length, along) - take_range(face_values, 0, length - 1, along)
    return result

def advance(radial_padded, azimuthal_padded, remapped, time_step):
    radial_div = direction_divergence(primitive(radial_padded), 0, (1, 2, 3))
    azimuthal_div = direction_divergence(primitive(azimuthal_padded), 1, (2, 3, 1))
    vertical_padded = jnp.concatenate([remapped[..., -2:], remapped, remapped[..., :2]], axis=3)
    vertical_div = direction_divergence(primitive(vertical_padded), 2, (3, 1, 2))
    gains = [0.0, 2.0 * OMEGA_RATE * remapped[2], -(2.0 - SHEAR_RATE) * OMEGA_RATE * remapped[1], 0.0, SHEAR_RATE * OMEGA_RATE * (remapped[1] * remapped[2] / remapped[0] - remapped[5] * remapped[6]), 0.0, -SHEAR_RATE * OMEGA_RATE * remapped[5], 0.0]
    outcome = []
    for component in range(8):
        change = radial_div[component] + azimuthal_div[component] + vertical_div[component]
        outcome.append(remapped[component] - time_step * change + time_step * gains[component])
    return jnp.stack(outcome)

def reference(fields, offsets, boundary_shift):
    radial_cells = fields.shape[1]
    loop_cells = fields.shape[2]
    depth_cells = fields.shape[3]
    amount = jnp.mod(offsets, loop_cells).astype(jnp.int32)
    positions = jnp.mod(jnp.arange(loop_cells, dtype=jnp.int32)[None, :] - amount[:, None], loop_cells).astype(jnp.int32)
    remapped_all = jnp.take_along_axis(fields, positions[None, :, :, None], axis=2)
    shear_cells = boundary_shift[0]
    lower_ghost = jnp.roll(remapped_all[:, radial_cells - 2:], shear_cells, axis=2)
    upper_ghost = jnp.roll(remapped_all[:, :2], -shear_cells, axis=2)
    radial_all = jnp.concatenate([lower_ghost, remapped_all, upper_ghost], axis=1)

    def block_peak(block_index):
        piece = lax.dynamic_slice_in_dim(fields, block_index * CX, CX, axis=1)
        return jnp.max(cell_speed(primitive(piece)))
    block_indices = jnp.arange(N_RAD, dtype=jnp.int32)
    global_peak = jnp.max(lax.map(block_peak, block_indices))
    time_step = CFL_NUMBER / global_peak

    def block_update(block_index):
        window = lax.dynamic_slice_in_dim(radial_all, block_index * CX, CX + 4, axis=1)
        remapped = window[:, 2:CX + 2]
        azimuthal_padded = jnp.concatenate([remapped[:, :, -2:], remapped, remapped[:, :, :2]], axis=2)
        return advance(window, azimuthal_padded, remapped, time_step)
    blocks = lax.map(block_update, block_indices)
    return jnp.moveaxis(blocks, 1, 0).reshape(8, radial_cells, loop_cells, depth_cells)
```

```python
import jax
import jax.numpy as jnp
from jax import lax
from jax.sharding import PartitionSpec as P

GAMMA_RATIO = 5.0 / 3.0
CFL_NUMBER = 0.4
OMEGA_RATE = 1.0
SHEAR_RATE = 1.5


def primitive(state):
    density = state[0]
    inverse = 1.0 / density
    speed_x = state[1] * inverse
    speed_y = state[2] * inverse
    speed_z = state[3] * inverse
    kinetic = 0.5 * density * (speed_x * speed_x + speed_y * speed_y + speed_z * speed_z)
    magnetic = 0.5 * (state[5] * state[5] + state[6] * state[6] + state[7] * state[7])
    pressure = (GAMMA_RATIO - 1.0) * (state[4] - kinetic - magnetic)
    return (density, speed_x, speed_y, speed_z, pressure, state[5], state[6], state[7])


def fast_speed(density, pressure, normal_field, field_sq):
    sound = (GAMMA_RATIO * pressure + field_sq) / density
    spread = jnp.maximum(
        sound * sound
        - 4.0 * GAMMA_RATIO * pressure * normal_field * normal_field / (density * density),
        0.0,
    )
    return jnp.sqrt(0.5 * (sound + jnp.sqrt(spread)))


def cell_speed(primitives):
    field_sq = (
        primitives[5] * primitives[5]
        + primitives[6] * primitives[6]
        + primitives[7] * primitives[7]
    )
    total = jnp.abs(primitives[1]) + fast_speed(
        primitives[0], primitives[4], primitives[5], field_sq
    )
    total = (
        total
        + jnp.abs(primitives[2])
        + fast_speed(primitives[0], primitives[4], primitives[6], field_sq)
    )
    total = (
        total
        + jnp.abs(primitives[3])
        + fast_speed(primitives[0], primitives[4], primitives[7], field_sq)
    )
    return total


def minmod(first_diff, second_diff):
    return (
        0.5
        * (jnp.sign(first_diff) + jnp.sign(second_diff))
        * jnp.minimum(jnp.abs(first_diff), jnp.abs(second_diff))
    )


def take_range(values, start_at, stop_at, along):
    return lax.slice_in_dim(values, start_at, stop_at, axis=along)


def side_terms(values, normal_field):
    density, normal_speed, trans_speed, other_speed, pressure = (
        values[0],
        values[1],
        values[2],
        values[3],
        values[4],
    )
    trans_field, other_field = (values[6], values[7])
    field_sq = normal_field * normal_field + trans_field * trans_field + other_field * other_field
    total_press = pressure + 0.5 * field_sq
    energy = (
        pressure / (GAMMA_RATIO - 1.0)
        + 0.5
        * density
        * (normal_speed * normal_speed + trans_speed * trans_speed + other_speed * other_speed)
        + 0.5 * field_sq
    )
    field_work = normal_speed * normal_field + trans_speed * trans_field + other_speed * other_field
    conserved = (
        density,
        density * normal_speed,
        density * trans_speed,
        density * other_speed,
        energy,
        normal_field,
        trans_field,
        other_field,
    )
    fluxes = (
        density * normal_speed,
        density * normal_speed * normal_speed + total_press - normal_field * normal_field,
        density * normal_speed * trans_speed - normal_field * trans_field,
        density * normal_speed * other_speed - normal_field * other_field,
        (energy + total_press) * normal_speed - normal_field * field_work,
        jnp.zeros_like(density),
        trans_field * normal_speed - normal_field * trans_speed,
        other_field * normal_speed - normal_field * other_speed,
    )
    signal = fast_speed(density, pressure, normal_field, field_sq)
    return (conserved, fluxes, total_press, energy, field_work, signal)


def star_state(values, energy, total_press, field_work, normal_field, outer, middle, star_press):
    density, normal_speed, trans_speed, other_speed = (values[0], values[1], values[2], values[3])
    trans_field, other_field = (values[6], values[7])
    relative = outer - normal_speed
    distance = outer - middle
    star_density = density * relative / distance
    product = density * relative * distance
    divisor = jnp.maximum(product - normal_field * normal_field, 0.5 * product)
    trans_star = trans_speed - normal_field * trans_field * (middle - normal_speed) / divisor
    other_star = other_speed - normal_field * other_field * (middle - normal_speed) / divisor
    factor = (density * relative * relative - normal_field * normal_field) / divisor
    trans_bstar = trans_field * factor
    other_bstar = other_field * factor
    star_work = middle * normal_field + trans_star * trans_bstar + other_star * other_bstar
    star_energy = (
        relative * energy
        - total_press * normal_speed
        + star_press * middle
        + normal_field * (field_work - star_work)
    ) / distance
    return (star_density, trans_star, other_star, trans_bstar, other_bstar, star_work, star_energy)


def hlld_flux(left_values, right_values):
    normal_field = 0.5 * (left_values[5] + right_values[5])
    cons_left, flux_left, press_left, energy_left, work_left, signal_left = side_terms(
        left_values, normal_field
    )
    cons_right, flux_right, press_right, energy_right, work_right, signal_right = side_terms(
        right_values, normal_field
    )
    fastest = jnp.maximum(signal_left, signal_right)
    lower = jnp.minimum(left_values[1], right_values[1]) - fastest
    upper = jnp.maximum(left_values[1], right_values[1]) + fastest
    mass_left = left_values[0] * (lower - left_values[1])
    mass_right = right_values[0] * (upper - right_values[1])
    guess = (
        mass_right * right_values[1] - mass_left * left_values[1] - press_right + press_left
    ) / (mass_right - mass_left)
    margin = 0.1 * (upper - lower)
    middle = jnp.clip(guess, lower + margin, upper - margin)
    star_press = press_left + mass_left * (middle - left_values[1])
    dens_left, trans_left, other_left, tfield_left, ofield_left, swork_left, senergy_left = (
        star_state(
            left_values, energy_left, press_left, work_left, normal_field, lower, middle, star_press
        )
    )
    dens_right, trans_right, other_right, tfield_right, ofield_right, swork_right, senergy_right = (
        star_state(
            right_values,
            energy_right,
            press_right,
            work_right,
            normal_field,
            upper,
            middle,
            star_press,
        )
    )
    root_left = jnp.sqrt(dens_left)
    root_right = jnp.sqrt(dens_right)
    sign_field = jnp.sign(normal_field)
    root_sum = root_left + root_right
    trans_double = (
        root_left * trans_left
        + root_right * trans_right
        + (tfield_right - tfield_left) * sign_field
    ) / root_sum
    other_double = (
        root_left * other_left
        + root_right * other_right
        + (ofield_right - ofield_left) * sign_field
    ) / root_sum
    tfield_double = (
        root_left * tfield_right
        + root_right * tfield_left
        + root_left * root_right * (trans_right - trans_left) * sign_field
    ) / root_sum
    ofield_double = (
        root_left * ofield_right
        + root_right * ofield_left
        + root_left * root_right * (other_right - other_left) * sign_field
    ) / root_sum
    double_work = (
        middle * normal_field + trans_double * tfield_double + other_double * ofield_double
    )
    denergy_left = senergy_left - root_left * (swork_left - double_work) * sign_field
    denergy_right = senergy_right + root_right * (swork_right - double_work) * sign_field
    inner_left = middle - jnp.abs(normal_field) / root_left
    inner_right = middle + jnp.abs(normal_field) / root_right
    star_cons_left = (
        dens_left,
        dens_left * middle,
        dens_left * trans_left,
        dens_left * other_left,
        senergy_left,
        normal_field,
        tfield_left,
        ofield_left,
    )
    star_cons_right = (
        dens_right,
        dens_right * middle,
        dens_right * trans_right,
        dens_right * other_right,
        senergy_right,
        normal_field,
        tfield_right,
        ofield_right,
    )
    double_cons_left = (
        dens_left,
        dens_left * middle,
        dens_left * trans_double,
        dens_left * other_double,
        denergy_left,
        normal_field,
        tfield_double,
        ofield_double,
    )
    double_cons_right = (
        dens_right,
        dens_right * middle,
        dens_right * trans_double,
        dens_right * other_double,
        denergy_right,
        normal_field,
        tfield_double,
        ofield_double,
    )
    outcome = []
    for component in range(8):
        star_left = flux_left[component] + lower * (
            star_cons_left[component] - cons_left[component]
        )
        double_left = star_left + inner_left * (
            double_cons_left[component] - star_cons_left[component]
        )
        star_right = flux_right[component] + upper * (
            star_cons_right[component] - cons_right[component]
        )
        double_right = star_right + inner_right * (
            double_cons_right[component] - star_cons_right[component]
        )
        chosen = jnp.where(
            lower > 0,
            flux_left[component],
            jnp.where(
                inner_left > 0,
                star_left,
                jnp.where(
                    middle > 0,
                    double_left,
                    jnp.where(
                        inner_right > 0,
                        double_right,
                        jnp.where(upper > 0, star_right, flux_right[component]),
                    ),
                ),
            ),
        )
        outcome.append(chosen)
    outcome[5] = jnp.zeros_like(outcome[0])
    return outcome


def direction_divergence(primitives, along, normal_order):
    mapping = (
        0,
        normal_order[0],
        normal_order[1],
        normal_order[2],
        4,
        normal_order[0] + 4,
        normal_order[1] + 4,
        normal_order[2] + 4,
    )
    left_faces = []
    right_faces = []
    for component in range(8):
        values = primitives[mapping[component]]
        length = values.shape[along]
        cell_count = length - 4
        differences = take_range(values, 1, length, along) - take_range(
            values, 0, length - 1, along
        )
        slopes = minmod(
            take_range(differences, 0, length - 2, along),
            take_range(differences, 1, length - 1, along),
        )
        centres = take_range(values, 1, length - 1, along)
        left_faces.append(
            take_range(centres, 0, cell_count + 1, along)
            + 0.5 * take_range(slopes, 0, cell_count + 1, along)
        )
        right_faces.append(
            take_range(centres, 1, cell_count + 2, along)
            - 0.5 * take_range(slopes, 1, cell_count + 2, along)
        )
    face_fluxes = hlld_flux(left_faces, right_faces)
    result = [None] * 8
    for component in range(8):
        face_values = face_fluxes[component]
        length = face_values.shape[along]
        result[mapping[component]] = take_range(face_values, 1, length, along) - take_range(
            face_values, 0, length - 1, along
        )
    return result


def advance(radial_padded, azimuthal_padded, remapped, time_step):
    radial_div = direction_divergence(primitive(radial_padded), 0, (1, 2, 3))
    azimuthal_div = direction_divergence(primitive(azimuthal_padded), 1, (2, 3, 1))
    vertical_padded = jnp.concatenate([remapped[..., -2:], remapped, remapped[..., :2]], axis=3)
    vertical_div = direction_divergence(primitive(vertical_padded), 2, (3, 1, 2))
    gains = [
        0.0,
        2.0 * OMEGA_RATE * remapped[2],
        -(2.0 - SHEAR_RATE) * OMEGA_RATE * remapped[1],
        0.0,
        SHEAR_RATE
        * OMEGA_RATE
        * (remapped[1] * remapped[2] / remapped[0] - remapped[5] * remapped[6]),
        0.0,
        -SHEAR_RATE * OMEGA_RATE * remapped[5],
        0.0,
    ]
    outcome = []
    for component in range(8):
        change = radial_div[component] + azimuthal_div[component] + vertical_div[component]
        outcome.append(remapped[component] - time_step * change + time_step * gains[component])
    return jnp.stack(outcome)


def local(fields, offsets, boundary_shift):
    parts, rows, cells, depth = fields.shape
    azimuth_devices = lax.axis_size("az")
    radial_devices = lax.axis_size("rad")
    loop_cells = cells * azimuth_devices
    radial_cells = rows * radial_devices
    time_step = CFL_NUMBER / lax.pmax(jnp.max(cell_speed(primitive(fields))), ("az", "rad"))
    radial_index = lax.axis_index("rad")
    lowest = radial_index == 0
    highest = radial_index == radial_devices - 1
    shear_cells = boundary_shift[0]
    ghost = lax.ppermute(
        jnp.where(lowest, fields[:, :2], fields[:, rows - 2 :]),
        "rad",
        [(0, radial_devices - 1), (radial_devices - 1, 0)],
    )
    units = jnp.concatenate([fields, ghost], axis=1).reshape(parts * (rows + 2), cells, depth)
    share = units.shape[0] // azimuth_devices
    rings = lax.all_to_all(units, "az", 0, 1, tiled=True)
    slot = jnp.mod(lax.axis_index("az") * share + jnp.arange(share, dtype=jnp.int32), rows + 2)
    ghost_row = jnp.where(lowest, radial_cells - 2, 0) + slot - rows
    row = jnp.where(slot < rows, radial_index * rows + slot, ghost_row)
    extra = jnp.where(slot < rows, 0, jnp.where(lowest, shear_cells, -shear_cells))
    shift = jnp.take(offsets, row) + extra
    width = cells + 4
    columns = (
        jnp.arange(azimuth_devices, dtype=jnp.int32)[:, None] * cells
        - 2
        + jnp.arange(width, dtype=jnp.int32)[None, :]
    ).reshape(-1)
    positions = jnp.mod(columns[None, :] - shift[:, None], loop_cells)
    windows = jnp.take_along_axis(rings, positions[:, :, None], axis=1)
    landed = lax.all_to_all(windows, "az", 1, 0, tiled=True)
    landed = landed.reshape(parts, rows + 2, width, depth)
    azimuthal_padded = landed[:, :rows]
    forward = [(i, (i + 1) % radial_devices) for i in range(radial_devices)]
    backward = [(target, source) for source, target in forward]
    remapped = azimuthal_padded[:, :, 2 : cells + 2]
    spare = landed[:, rows:, 2 : cells + 2]
    low = lax.ppermute(remapped[:, rows - 2 :], "rad", forward)
    high = lax.ppermute(remapped[:, :2], "rad", backward)
    low = jnp.where(lowest, spare, low)
    high = jnp.where(highest, spare, high)
    radial_padded = jnp.concatenate([low, remapped, high], axis=1)
    return advance(radial_padded, azimuthal_padded, remapped, time_step)


def solution(mesh):
    in_specs = (P(None, "rad", "az", None), P(), P())
    out_specs = P(None, "rad", "az", None)
    return jax.shard_map(local, mesh=mesh, in_specs=in_specs, out_specs=out_specs, check_vma=False)
```

```python
import functools

import jax
import jax.numpy as jnp
from jax import lax
from jax.experimental import pallas as pl
from jax.experimental.pallas import tpu as pltpu
from jax.sharding import PartitionSpec as P

GAMMA_RATIO = 5.0 / 3.0
CFL_NUMBER = 0.4
OMEGA_RATE = 1.0
SHEAR_RATE = 1.5


def primitive(state):
    density = state[0]
    inverse = 1.0 / density
    speed_x = state[1] * inverse
    speed_y = state[2] * inverse
    speed_z = state[3] * inverse
    kinetic = 0.5 * density * (speed_x * speed_x + speed_y * speed_y + speed_z * speed_z)
    magnetic = 0.5 * (state[5] * state[5] + state[6] * state[6] + state[7] * state[7])
    pressure = (GAMMA_RATIO - 1.0) * (state[4] - kinetic - magnetic)
    return (density, speed_x, speed_y, speed_z, pressure, state[5], state[6], state[7])


def fast_speed(density, pressure, normal_field, field_sq):
    sound = (GAMMA_RATIO * pressure + field_sq) / density
    spread = jnp.maximum(
        sound * sound
        - 4.0 * GAMMA_RATIO * pressure * normal_field * normal_field / (density * density),
        0.0,
    )
    return jnp.sqrt(0.5 * (sound + jnp.sqrt(spread)))


def cell_speed(primitives):
    field_sq = (
        primitives[5] * primitives[5]
        + primitives[6] * primitives[6]
        + primitives[7] * primitives[7]
    )
    total = jnp.abs(primitives[1]) + fast_speed(
        primitives[0], primitives[4], primitives[5], field_sq
    )
    total = (
        total
        + jnp.abs(primitives[2])
        + fast_speed(primitives[0], primitives[4], primitives[6], field_sq)
    )
    total = (
        total
        + jnp.abs(primitives[3])
        + fast_speed(primitives[0], primitives[4], primitives[7], field_sq)
    )
    return total


ADIABATIC = 1.0 / (GAMMA_RATIO - 1.0)
ORDERS = ((1, 2, 3), (2, 3, 1), (3, 1, 2))
MARGIN = 8


def inverse_of(values):
    return 1.0 / values


def half_slope(first_diff, second_diff):
    return 0.5 * (
        jnp.maximum(jnp.minimum(first_diff, second_diff), 0.0)
        + jnp.minimum(jnp.maximum(first_diff, second_diff), 0.0)
    )


def half_square_speed(density, pressure, normal_sq, field_sq):
    inverse = inverse_of(density)
    sound = (GAMMA_RATIO * pressure + field_sq) * inverse
    spread = sound * sound - (4.0 * GAMMA_RATIO) * pressure * normal_sq * (inverse * inverse)
    return 0.5 * (sound + jnp.sqrt(jnp.maximum(spread, 0.0)))


def star_part(values, mass, gap, outer, middle, bn, bn_sq):
    distance = outer - middle
    inverse = inverse_of(distance)
    density = mass * inverse
    product = mass * distance
    divisor = inverse_of(jnp.maximum(product - bn_sq, 0.5 * product))
    turn = bn * (middle - values[1]) * divisor
    factor = (mass * gap - bn_sq) * divisor
    root_inverse = lax.rsqrt(density)
    return (
        density,
        values[2] - values[6] * turn,
        values[3] - values[7] * turn,
        values[6] * factor,
        values[7] * factor,
        inverse,
        density * root_inverse,
        root_inverse,
    )


def face_flux(left, right):
    bn = 0.5 * (left[5] + right[5])
    bn_sq = bn * bn
    sq_left = bn_sq + left[6] * left[6] + left[7] * left[7]
    sq_right = bn_sq + right[6] * right[6] + right[7] * right[7]
    fastest = jnp.sqrt(
        jnp.maximum(
            half_square_speed(left[0], left[4], bn_sq, sq_left),
            half_square_speed(right[0], right[4], bn_sq, sq_right),
        )
    )
    lower = jnp.minimum(left[1], right[1]) - fastest
    upper = jnp.maximum(left[1], right[1]) + fastest
    gap_left = lower - left[1]
    gap_right = upper - right[1]
    mass_left = left[0] * gap_left
    mass_right = right[0] * gap_right
    press_left = left[4] + 0.5 * sq_left
    press_right = right[4] + 0.5 * sq_right
    guess = (
        mass_right * right[1] - mass_left * left[1] - press_right + press_left
    ) * inverse_of(mass_right - mass_left)
    margin = 0.1 * (upper - lower)
    middle = jnp.minimum(jnp.maximum(guess, lower + margin), upper - margin)
    star_press = press_left + mass_left * (middle - left[1])
    star_left = star_part(left, mass_left, gap_left, lower, middle, bn, bn_sq)
    star_right = star_part(right, mass_right, gap_right, upper, middle, bn, bn_sq)
    sign = jnp.where(bn > 0.0, 1.0, jnp.where(bn < 0.0, -1.0, 0.0))
    root_left, root_right = star_left[6], star_right[6]
    share = inverse_of(root_left + root_right)
    share_left = root_left * share
    share_right = root_right * share
    kick = sign * share
    cross = root_left * share_right * sign
    v_double = (
        share_left * star_left[1]
        + share_right * star_right[1]
        + (star_right[3] - star_left[3]) * kick
    )
    w_double = (
        share_left * star_left[2]
        + share_right * star_right[2]
        + (star_right[4] - star_left[4]) * kick
    )
    bt_double = (
        share_left * star_right[3]
        + share_right * star_left[3]
        + (star_right[1] - star_left[1]) * cross
    )
    bw_double = (
        share_left * star_right[4]
        + share_right * star_left[4]
        + (star_right[2] - star_left[2]) * cross
    )
    on_left = middle > 0.0

    def pick(first, second):
        return jnp.where(on_left, first, second)

    rho, u, v, w, p, bt, bw = (pick(left[c], right[c]) for c in (0, 1, 2, 3, 4, 6, 7))
    pt = pick(press_left, press_right)
    outer = pick(lower, upper)
    gap = pick(gap_left, gap_right)
    rho_s, v_s, w_s, bt_s, bw_s, inv_s, root_s, root_inv = (
        pick(a, b) for a, b in zip(star_left, star_right)
    )
    energy = (ADIABATIC - 1.0) * p + pt + 0.5 * rho * (u * u + v * v + w * w)
    work = u * bn + v * bt + w * bw
    middle_work = middle * bn
    work_s = middle_work + v_s * bt_s + w_s * bw_s
    work_d = middle_work + v_double * bt_double + w_double * bw_double
    energy_s = (gap * energy - pt * u + star_press * middle + bn * (work - work_s)) * inv_s
    side = pick(sign, -sign)
    energy_step = side * root_s * (work_d - work_s)
    alfven = jnp.abs(bn) * root_inv
    inner = middle - pick(alfven, -alfven)
    outer_on = outer > 0.0
    inner_on = inner > 0.0
    first = jnp.where(
        on_left, jnp.where(outer_on, 0.0, outer), jnp.where(inner_on | outer_on, outer, 0.0)
    )
    second = jnp.where(
        on_left, jnp.where(outer_on | inner_on, 0.0, inner), jnp.where(inner_on, inner, 0.0)
    )
    momentum = rho * u
    second_mass = second * rho_s
    return (
        momentum + first * (rho_s - rho),
        momentum * u + pt - bn_sq + first * (rho_s * middle - momentum),
        momentum * v - bn * bt + first * (rho_s * v_s - rho * v) + second_mass * (v_double - v_s),
        momentum * w - bn * bw + first * (rho_s * w_s - rho * w) + second_mass * (w_double - w_s),
        (energy + pt) * u - bn * work + first * (energy_s - energy) + second * energy_step,
        bt * u - bn * v + first * (bt_s - bt) + second * (bt_double - bt_s),
        bw * u - bn * w + first * (bw_s - bw) + second * (bw_double - bw_s),
    )


def targets(order):
    return (0, order[0], order[1], order[2], 4, order[1] + 4, order[2] + 4)


def sources(order):
    return (0, order[0], order[1], order[2], 4, order[0] + 4, order[1] + 4, order[2] + 4)


def faces_between(before, here, after, beyond):
    middle_diff = after - here
    return (
        here + half_slope(here - before, middle_diff),
        after - half_slope(middle_diff, beyond - after),
    )


def flux_between(read, order):
    pairs = [faces_between(*read(c)) for c in sources(order)]
    return face_flux([pair[0] for pair in pairs], [pair[1] for pair in pairs])


def flux_kernel(landed, low, high, step, out, prims, radial_flux, ring_flux):
    rows, cells = out.shape[1], out.shape[2]
    depth = out.shape[3]
    chunks = cells // 8
    dt = step[0]

    def fill(i, _):
        values = primitive([landed[f, i] for f in range(8)])
        for f in range(8):
            prims[f, i + 2, MARGIN - 2 : MARGIN + cells + 2] = values[f]
        return 0

    lax.fori_loop(0, rows, fill, 0)
    for g in range(2):
        for ref, row in ((low, g), (high, rows + 2 + g)):
            values = primitive([ref[f, g] for f in range(8)])
            for f in range(8):
                prims[f, row, MARGIN : MARGIN + cells] = values[f]

    def radial(row, q):
        columns = slice(MARGIN + 8 * q, MARGIN + 8 * q + 8)
        return flux_between(
            lambda c: [prims[c, row + near, columns] for near in (-1, 0, 1, 2)], ORDERS[0]
        )

    for q in range(chunks):
        for c, value in enumerate(radial(1, q)):
            radial_flux[c, 8 * q : 8 * q + 8] = value

    def advance_row(i, _):
        row = i + 2
        for q in range(chunks + 1):
            begin = MARGIN - 1 + 8 * q
            fluxes = flux_between(
                lambda c: [
                    prims[c, row, begin + near : begin + near + 8] for near in (-1, 0, 1, 2)
                ],
                ORDERS[1],
            )
            for c, value in enumerate(fluxes):
                ring_flux[c, 8 * q : 8 * q + 8] = value
        for q in range(chunks):
            inside = slice(8 * q, 8 * q + 8)
            columns = slice(MARGIN + 8 * q, MARGIN + 8 * q + 8)
            change = [None] * 8

            def gather(order, values):
                for c, value in zip(targets(order), values):
                    change[c] = value if change[c] is None else change[c] + value

            upper = radial(row, q)
            gather(ORDERS[0], [value - radial_flux[c, inside] for c, value in enumerate(upper)])
            for c, value in enumerate(upper):
                radial_flux[c, inside] = value
            gather(
                ORDERS[1],
                [ring_flux[c, 8 * q + 1 : 8 * q + 9] - ring_flux[c, inside] for c in range(7)],
            )
            lefts, rights = [], []
            for c in sources(ORDERS[2]):
                here = prims[c, row, columns]
                diff = pltpu.roll(here, depth - 1, 1) - here
                slope = half_slope(pltpu.roll(diff, 1, 1), diff)
                lefts.append(here + slope)
                rights.append(pltpu.roll(here - slope, depth - 1, 1))
            above = face_flux(lefts, rights)
            gather(ORDERS[2], [value - pltpu.roll(value, 1, 1) for value in above])
            state = [landed[f, i, 8 * q + 2 : 8 * q + 10] for f in range(8)]
            speed_x = prims[1, row, columns]
            gains = {
                1: (2.0 * OMEGA_RATE) * state[2],
                2: (-(2.0 - SHEAR_RATE) * OMEGA_RATE) * state[1],
                4: (SHEAR_RATE * OMEGA_RATE) * (speed_x * state[2] - state[5] * state[6]),
                6: (-SHEAR_RATE * OMEGA_RATE) * state[5],
            }
            for f in range(8):
                total = gains[f] - change[f] if f in gains else -change[f]
                out[f, i, inside] = state[f] + dt * total
        return 0

    lax.fori_loop(0, rows, advance_row, 0)


def advanced(landed, low, high, time_step, rows, cells):
    parts, depth = landed.shape[0], landed.shape[3]
    vmem = pl.BlockSpec(memory_space=pltpu.VMEM)
    return pl.pallas_call(
        flux_kernel,
        out_shape=jax.ShapeDtypeStruct((parts, rows, cells, depth), jnp.float32),
        in_specs=[vmem, vmem, vmem, pl.BlockSpec(memory_space=pltpu.SMEM)],
        out_specs=vmem,
        scratch_shapes=[
            pltpu.VMEM((parts, rows + 4, cells + 3 * MARGIN, depth), jnp.float32),
            pltpu.VMEM((7, cells, depth), jnp.float32),
            pltpu.VMEM((7, cells + 8, depth), jnp.float32),
        ],
        compiler_params=pltpu.CompilerParams(vmem_limit_bytes=40 * 1024 * 1024),
        name="advance",
    )(landed, low, high, time_step.reshape(1))


def turn_kernel(count, shifts, ring, out, doubled):
    loop_cells = ring.shape[1]
    cells = loop_cells // count
    width = out.shape[2]
    doubled[:loop_cells] = ring[0]
    doubled[loop_cells : loop_cells + width] = ring[0, :width]
    shift = shifts[pl.program_id(0)]
    for t in range(count):
        start = lax.rem(t * cells - 2 - shift + 4 * loop_cells, loop_cells)
        out[0, t] = doubled[pl.ds(start, width)]


def turned(rings, shift, count):
    share, loop_cells, depth = rings.shape
    width = loop_cells // count + 4
    return pl.pallas_call(
        functools.partial(turn_kernel, count),
        out_shape=jax.ShapeDtypeStruct((share, count, width, depth), jnp.float32),
        grid_spec=pltpu.PrefetchScalarGridSpec(
            num_scalar_prefetch=1,
            grid=(share,),
            in_specs=[pl.BlockSpec((1, loop_cells, depth), lambda u, s: (u, 0, 0))],
            out_specs=pl.BlockSpec((1, count, width, depth), lambda u, s: (u, 0, 0, 0)),
            scratch_shapes=[pltpu.VMEM((loop_cells + width + 4, depth), jnp.float32)],
        ),
        name="turn",
    )(shift, rings)


def local(fields, offsets, boundary_shift):
    parts, rows, cells, depth = fields.shape
    azimuth_devices = lax.axis_size("az")
    radial_devices = lax.axis_size("rad")
    loop_cells = cells * azimuth_devices
    radial_cells = rows * radial_devices
    time_step = CFL_NUMBER / lax.pmax(jnp.max(cell_speed(primitive(fields))), ("az", "rad"))
    radial_index = lax.axis_index("rad")
    lowest = radial_index == 0
    highest = radial_index == radial_devices - 1
    shear_cells = boundary_shift[0]
    ghost = lax.ppermute(
        jnp.where(lowest, fields[:, :2], fields[:, rows - 2 :]),
        "rad",
        [(0, radial_devices - 1), (radial_devices - 1, 0)],
    )
    units = jnp.concatenate([fields, ghost], axis=1).reshape(parts * (rows + 2), cells, depth)
    share = units.shape[0] // azimuth_devices
    rings = lax.all_to_all(units, "az", 0, 1, tiled=True)
    slot = jnp.mod(lax.axis_index("az") * share + jnp.arange(share, dtype=jnp.int32), rows + 2)
    ghost_row = jnp.where(lowest, radial_cells - 2, 0) + slot - rows
    row = jnp.where(slot < rows, radial_index * rows + slot, ghost_row)
    extra = jnp.where(slot < rows, 0, jnp.where(lowest, shear_cells, -shear_cells))
    shift = jnp.take(offsets, row) + extra
    windows = turned(rings, jnp.mod(shift, loop_cells), azimuth_devices)
    landed = lax.all_to_all(windows, "az", 1, 0, tiled=True)
    landed = landed.reshape(parts, rows + 2, cells + 4, depth)
    forward = [(i, (i + 1) % radial_devices) for i in range(radial_devices)]
    backward = [(target, source) for source, target in forward]
    spare = landed[:, rows:, 2 : cells + 2]
    low = lax.ppermute(landed[:, rows - 2 : rows, 2 : cells + 2], "rad", forward)
    high = lax.ppermute(landed[:, :2, 2 : cells + 2], "rad", backward)
    low = jnp.where(lowest, spare, low)
    high = jnp.where(highest, spare, high)
    return advanced(landed, low, high, time_step, rows, cells)


def solution(mesh):
    in_specs = (P(None, "rad", "az", None), P(), P())
    out_specs = P(None, "rad", "az", None)
    return jax.shard_map(local, mesh=mesh, in_specs=in_specs, out_specs=out_specs, check_vma=False)
```

```python
import functools

import jax
import jax.numpy as jnp
from jax import lax
from jax.experimental import pallas as pl
from jax.experimental.pallas import tpu as pltpu
from jax.sharding import PartitionSpec as P

GAMMA_RATIO = 5.0 / 3.0
CFL_NUMBER = 0.4
OMEGA_RATE = 1.0
SHEAR_RATE = 1.5


def primitive(state):
    density = state[0]
    inverse = 1.0 / density
    speed_x = state[1] * inverse
    speed_y = state[2] * inverse
    speed_z = state[3] * inverse
    kinetic = 0.5 * density * (speed_x * speed_x + speed_y * speed_y + speed_z * speed_z)
    magnetic = 0.5 * (state[5] * state[5] + state[6] * state[6] + state[7] * state[7])
    pressure = (GAMMA_RATIO - 1.0) * (state[4] - kinetic - magnetic)
    return (density, speed_x, speed_y, speed_z, pressure, state[5], state[6], state[7])


def fast_speed(density, pressure, normal_field, field_sq):
    sound = (GAMMA_RATIO * pressure + field_sq) / density
    spread = jnp.maximum(
        sound * sound
        - 4.0 * GAMMA_RATIO * pressure * normal_field * normal_field / (density * density),
        0.0,
    )
    return jnp.sqrt(0.5 * (sound + jnp.sqrt(spread)))


def cell_speed(primitives):
    field_sq = (
        primitives[5] * primitives[5]
        + primitives[6] * primitives[6]
        + primitives[7] * primitives[7]
    )
    total = jnp.abs(primitives[1]) + fast_speed(
        primitives[0], primitives[4], primitives[5], field_sq
    )
    total = (
        total
        + jnp.abs(primitives[2])
        + fast_speed(primitives[0], primitives[4], primitives[6], field_sq)
    )
    total = (
        total
        + jnp.abs(primitives[3])
        + fast_speed(primitives[0], primitives[4], primitives[7], field_sq)
    )
    return total


ADIABATIC = 1.0 / (GAMMA_RATIO - 1.0)
ORDERS = ((1, 2, 3), (2, 3, 1), (3, 1, 2))
MARGIN = 8


def inverse_of(values):
    return 1.0 / values


def half_slope(first_diff, second_diff):
    return 0.5 * (
        jnp.maximum(jnp.minimum(first_diff, second_diff), 0.0)
        + jnp.minimum(jnp.maximum(first_diff, second_diff), 0.0)
    )


def half_square_speed(density, pressure, normal_sq, field_sq):
    inverse = inverse_of(density)
    sound = (GAMMA_RATIO * pressure + field_sq) * inverse
    spread = sound * sound - (4.0 * GAMMA_RATIO) * pressure * normal_sq * (inverse * inverse)
    return 0.5 * (sound + jnp.sqrt(jnp.maximum(spread, 0.0)))


def star_part(values, mass, gap, outer, middle, bn, bn_sq):
    distance = outer - middle
    inverse = inverse_of(distance)
    density = mass * inverse
    product = mass * distance
    divisor = inverse_of(jnp.maximum(product - bn_sq, 0.5 * product))
    turn = bn * (middle - values[1]) * divisor
    factor = (mass * gap - bn_sq) * divisor
    root_inverse = lax.rsqrt(density)
    return (
        density,
        values[2] - values[6] * turn,
        values[3] - values[7] * turn,
        values[6] * factor,
        values[7] * factor,
        inverse,
        density * root_inverse,
        root_inverse,
    )


def face_flux(left, right):
    bn = 0.5 * (left[5] + right[5])
    bn_sq = bn * bn
    sq_left = bn_sq + left[6] * left[6] + left[7] * left[7]
    sq_right = bn_sq + right[6] * right[6] + right[7] * right[7]
    fastest = jnp.sqrt(
        jnp.maximum(
            half_square_speed(left[0], left[4], bn_sq, sq_left),
            half_square_speed(right[0], right[4], bn_sq, sq_right),
        )
    )
    lower = jnp.minimum(left[1], right[1]) - fastest
    upper = jnp.maximum(left[1], right[1]) + fastest
    gap_left = lower - left[1]
    gap_right = upper - right[1]
    mass_left = left[0] * gap_left
    mass_right = right[0] * gap_right
    press_left = left[4] + 0.5 * sq_left
    press_right = right[4] + 0.5 * sq_right
    guess = (
        mass_right * right[1] - mass_left * left[1] - press_right + press_left
    ) * inverse_of(mass_right - mass_left)
    margin = 0.1 * (upper - lower)
    middle = jnp.minimum(jnp.maximum(guess, lower + margin), upper - margin)
    star_press = press_left + mass_left * (middle - left[1])
    star_left = star_part(left, mass_left, gap_left, lower, middle, bn, bn_sq)
    star_right = star_part(right, mass_right, gap_right, upper, middle, bn, bn_sq)
    sign = jnp.where(bn > 0.0, 1.0, jnp.where(bn < 0.0, -1.0, 0.0))
    root_left, root_right = star_left[6], star_right[6]
    share = inverse_of(root_left + root_right)
    share_left = root_left * share
    share_right = root_right * share
    kick = sign * share
    cross = root_left * share_right * sign
    v_double = (
        share_left * star_left[1]
        + share_right * star_right[1]
        + (star_right[3] - star_left[3]) * kick
    )
    w_double = (
        share_left * star_left[2]
        + share_right * star_right[2]
        + (star_right[4] - star_left[4]) * kick
    )
    bt_double = (
        share_left * star_right[3]
        + share_right * star_left[3]
        + (star_right[1] - star_left[1]) * cross
    )
    bw_double = (
        share_left * star_right[4]
        + share_right * star_left[4]
        + (star_right[2] - star_left[2]) * cross
    )
    on_left = middle > 0.0

    def pick(first, second):
        return jnp.where(on_left, first, second)

    rho, u, v, w, p, bt, bw = (pick(left[c], right[c]) for c in (0, 1, 2, 3, 4, 6, 7))
    pt = pick(press_left, press_right)
    outer = pick(lower, upper)
    gap = pick(gap_left, gap_right)
    rho_s, v_s, w_s, bt_s, bw_s, inv_s, root_s, root_inv = (
        pick(a, b) for a, b in zip(star_left, star_right)
    )
    energy = (ADIABATIC - 1.0) * p + pt + 0.5 * rho * (u * u + v * v + w * w)
    work = u * bn + v * bt + w * bw
    middle_work = middle * bn
    work_s = middle_work + v_s * bt_s + w_s * bw_s
    work_d = middle_work + v_double * bt_double + w_double * bw_double
    energy_s = (gap * energy - pt * u + star_press * middle + bn * (work - work_s)) * inv_s
    side = pick(sign, -sign)
    energy_step = side * root_s * (work_d - work_s)
    alfven = jnp.abs(bn) * root_inv
    inner = middle - pick(alfven, -alfven)
    outer_on = outer > 0.0
    inner_on = inner > 0.0
    first = jnp.where(
        on_left, jnp.where(outer_on, 0.0, outer), jnp.where(inner_on | outer_on, outer, 0.0)
    )
    second = jnp.where(
        on_left, jnp.where(outer_on | inner_on, 0.0, inner), jnp.where(inner_on, inner, 0.0)
    )
    momentum = rho * u
    second_mass = second * rho_s
    return (
        momentum + first * (rho_s - rho),
        momentum * u + pt - bn_sq + first * (rho_s * middle - momentum),
        momentum * v - bn * bt + first * (rho_s * v_s - rho * v) + second_mass * (v_double - v_s),
        momentum * w - bn * bw + first * (rho_s * w_s - rho * w) + second_mass * (w_double - w_s),
        (energy + pt) * u - bn * work + first * (energy_s - energy) + second * energy_step,
        bt * u - bn * v + first * (bt_s - bt) + second * (bt_double - bt_s),
        bw * u - bn * w + first * (bw_s - bw) + second * (bw_double - bw_s),
    )


def targets(order):
    return (0, order[0], order[1], order[2], 4, order[1] + 4, order[2] + 4)


def sources(order):
    return (0, order[0], order[1], order[2], 4, order[0] + 4, order[1] + 4, order[2] + 4)


def faces_between(before, here, after, beyond):
    middle_diff = after - here
    return (
        here + half_slope(here - before, middle_diff),
        after - half_slope(middle_diff, beyond - after),
    )


def flux_between(read, order):
    pairs = [faces_between(*read(c)) for c in sources(order)]
    return face_flux([pair[0] for pair in pairs], [pair[1] for pair in pairs])


def flux_kernel(landed, low, high, peaks, out, prims, radial_flux, ring_flux):
    rows, cells = out.shape[1], out.shape[2]
    depth = out.shape[3]
    chunks = cells // 8
    dt = CFL_NUMBER / jnp.max(peaks[...])

    def fill(i, _):
        values = primitive([landed[f, i] for f in range(8)])
        for f in range(8):
            prims[f, i + 2, MARGIN - 2 : MARGIN + cells + 2] = values[f]
        return 0

    lax.fori_loop(0, rows, fill, 0)
    for g in range(2):
        for ref, row in ((low, g), (high, rows + 2 + g)):
            values = primitive([ref[f, g] for f in range(8)])
            for f in range(8):
                prims[f, row, MARGIN - 2 : MARGIN + cells + 2] = values[f]

    def radial(row, q):
        columns = slice(MARGIN + 8 * q, MARGIN + 8 * q + 8)
        return flux_between(
            lambda c: [prims[c, row + near, columns] for near in (-1, 0, 1, 2)], ORDERS[0]
        )

    for q in range(chunks):
        for c, value in enumerate(radial(1, q)):
            radial_flux[c, 8 * q : 8 * q + 8] = value

    def advance_row(i, _):
        row = i + 2
        for q in range(chunks + 1):
            begin = MARGIN - 1 + 8 * q
            fluxes = flux_between(
                lambda c: [
                    prims[c, row, begin + near : begin + near + 8] for near in (-1, 0, 1, 2)
                ],
                ORDERS[1],
            )
            for c, value in enumerate(fluxes):
                ring_flux[c, 8 * q : 8 * q + 8] = value
        for q in range(chunks):
            inside = slice(8 * q, 8 * q + 8)
            columns = slice(MARGIN + 8 * q, MARGIN + 8 * q + 8)
            change = [None] * 8

            def gather(order, values):
                for c, value in zip(targets(order), values):
                    change[c] = value if change[c] is None else change[c] + value

            upper = radial(row, q)
            gather(ORDERS[0], [value - radial_flux[c, inside] for c, value in enumerate(upper)])
            for c, value in enumerate(upper):
                radial_flux[c, inside] = value
            gather(
                ORDERS[1],
                [ring_flux[c, 8 * q + 1 : 8 * q + 9] - ring_flux[c, inside] for c in range(7)],
            )
            lefts, rights = [], []
            for c in sources(ORDERS[2]):
                here = prims[c, row, columns]
                diff = pltpu.roll(here, depth - 1, 1) - here
                slope = half_slope(pltpu.roll(diff, 1, 1), diff)
                lefts.append(here + slope)
                rights.append(pltpu.roll(here - slope, depth - 1, 1))
            above = face_flux(lefts, rights)
            gather(ORDERS[2], [value - pltpu.roll(value, 1, 1) for value in above])
            state = [landed[f, i, 8 * q + 2 : 8 * q + 10] for f in range(8)]
            speed_x = prims[1, row, columns]
            gains = {
                1: (2.0 * OMEGA_RATE) * state[2],
                2: (-(2.0 - SHEAR_RATE) * OMEGA_RATE) * state[1],
                4: (SHEAR_RATE * OMEGA_RATE) * (speed_x * state[2] - state[5] * state[6]),
                6: (-SHEAR_RATE * OMEGA_RATE) * state[5],
            }
            for f in range(8):
                total = gains[f] - change[f] if f in gains else -change[f]
                out[f, i, inside] = state[f] + dt * total
        return 0

    lax.fori_loop(0, rows, advance_row, 0)


def advanced(landed, low, high, peaks, rows, cells):
    parts, depth = landed.shape[0], landed.shape[3]
    vmem = pl.BlockSpec(memory_space=pltpu.VMEM)
    return pl.pallas_call(
        flux_kernel,
        out_shape=jax.ShapeDtypeStruct((parts, rows, cells, depth), jnp.float32),
        in_specs=[vmem] * 4,
        out_specs=vmem,
        scratch_shapes=[
            pltpu.VMEM((parts, rows + 4, cells + 3 * MARGIN, depth), jnp.float32),
            pltpu.VMEM((7, cells, depth), jnp.float32),
            pltpu.VMEM((7, cells + 8, depth), jnp.float32),
        ],
        compiler_params=pltpu.CompilerParams(vmem_limit_bytes=40 * 1024 * 1024),
        name="advance",
    )(landed, low, high, peaks)


CHUNKS = 4


def exchange_kernel(
    rows, az_count, rad_count,
    fields, offsets, shear,
    landed, low, high, rad_peaks,
    ghosts, windows, ghost_send, ghost_land, low_send, high_send, low_land, high_land, az_peaks,
    *rest,
):
    rings = rest[: CHUNKS + 1]
    out_send, out_recv, back_send, back_recv, rad_send, rad_recv, peak_send, peak_recv = rest[
        CHUNKS + 1 : CHUNKS + 9
    ]
    barrier = pltpu.get_barrier_semaphore()
    az = lax.axis_index("az")
    rad = lax.axis_index("rad")
    cells = fields.shape[1]
    width = landed.shape[1]
    loop_cells = cells * az_count
    radial_cells = rows * rad_count
    parts = fields.shape[0] // rows
    main = fields.shape[0] // az_count
    spare = 2 * parts // az_count
    piece = main // CHUNKS
    lowest = rad == 0
    highest = rad == rad_count - 1

    def az_peer(k):
        return lax.rem(az + k, az_count)

    def rad_peer(k):
        return lax.rem(rad + k, rad_count)

    for k in range(1, az_count):
        pl.semaphore_signal(
            barrier, inc=1, device_id=(az_peer(k), rad), device_id_type=pl.DeviceIdType.MESH
        )
    for k in range(1, rad_count):
        pl.semaphore_signal(
            barrier, inc=1, device_id=(az, rad_peer(k)), device_id_type=pl.DeviceIdType.MESH
        )
    pl.semaphore_wait(barrier, az_count + rad_count - 2)

    def remote(src, dst, send, recv, target):
        return pltpu.make_async_remote_copy(
            src_ref=src,
            dst_ref=dst,
            send_sem=send,
            recv_sem=recv,
            device_id=target,
            device_id_type=pl.DeviceIdType.MESH,
        )

    for f in range(parts):
        for g in range(2):
            edge = jnp.where(lowest, g, rows - 2 + g)
            ghost_send[2 * f + g] = fields[f * rows + edge]
    ghost_copy = remote(
        ghost_send, ghost_land, rad_send.at[0], rad_recv.at[0], (az, rad_count - 1 - rad)
    )
    ghost_copy.start()

    own = pl.ds(pl.multiple_of(az * cells, cells), cells)

    def outward(c, k):
        peer = az_peer(k)
        if c < CHUNKS:
            src = fields.at[pl.ds(peer * main + c * piece, piece)]
        else:
            src = ghost_land.at[pl.ds(peer * spare, spare)]
        return remote(
            src, rings[c].at[:, own], out_send.at[c, k], out_recv.at[c, k], (peer, rad)
        )

    sends = []
    for c in range(CHUNKS):
        for k in range(1, az_count):
            sends.append(outward(c, k))
            sends[-1].start()
    ghost_copy.wait()
    for k in range(1, az_count):
        sends.append(outward(CHUNKS, k))
        sends[-1].start()
    for c in range(CHUNKS):
        rings[c][:, own] = fields[pl.ds(az * main + c * piece, piece)]
    rings[CHUNKS][:, own] = ghost_land[pl.ds(az * spare, spare)]

    def peak_of(i, best):
        return jnp.maximum(
            best, cell_speed(primitive([fields[f * rows + i] for f in range(parts)]))
        )

    best = lax.fori_loop(0, rows, peak_of, jnp.zeros(fields.shape[1:], jnp.float32))
    tile = best[:8]
    for q in range(1, cells // 8):
        tile = jnp.maximum(tile, best[8 * q : 8 * q + 8])
    az_peaks[az] = tile
    peak_copies = []
    for k in range(1, az_count):
        peak_copies.append(
            remote(
                az_peaks.at[az],
                az_peaks.at[az],
                peak_send.at[k],
                peak_recv.at[k],
                (az_peer(k), rad),
            )
        )
        peak_copies[-1].start()

    returns = []

    def backward(first, count, place, c, k):
        peer = az_peer(k)
        return remote(
            windows.at[peer, pl.ds(first, count)],
            place,
            back_send.at[c, k],
            back_recv.at[c, k],
            (peer, rad),
        )

    for c in range(CHUNKS + 1):
        for k in range(1, az_count):
            outward(c, k).wait_recv()
        count = piece if c < CHUNKS else spare
        first = c * piece
        ring = rings[c]
        for u in range(count):
            ring[u, loop_cells : loop_cells + width + 4] = ring[u, : width + 4]
        for u in range(count):
            if c < CHUNKS:
                row = rad * rows + lax.rem(az * main + first + u, rows)
                shift = offsets[row]
            else:
                g = lax.rem(az * spare + u, 2)
                row = jnp.where(lowest, radial_cells - 2, 0) + g
                shift = offsets[row] + jnp.where(lowest, shear[0], -shear[0])
            for t in range(az_count):
                start = lax.rem(t * cells - 2 - shift + 4 * loop_cells, loop_cells)
                windows[t, first + u] = ring[u, pl.ds(start, width)]
        if c < CHUNKS:
            place = landed.at[pl.ds(az * main + first, count)]
        else:
            place = ghosts.at[pl.ds(az * spare, count)]
        for k in range(1, az_count):
            returns.append(backward(first, count, place, c, k))
            returns[-1].start()
        if c < CHUNKS:
            landed[pl.ds(az * main + first, count)] = windows[az, first : first + count]
        else:
            ghosts[pl.ds(az * spare, count)] = windows[az, first : first + count]

    for copy in peak_copies:
        copy.wait_recv()
    tile = az_peaks[0]
    for a in range(1, az_count):
        tile = jnp.maximum(tile, az_peaks[a])
    rad_peaks[rad] = tile
    for k in range(1, rad_count):
        copy = remote(
            rad_peaks.at[rad],
            rad_peaks.at[rad],
            peak_send.at[az_count + k],
            peak_recv.at[az_count + k],
            (az, rad_peer(k)),
        )
        peak_copies.append(copy)
        copy.start()

    for copy in returns:
        copy.wait_recv()
    for f in range(parts):
        for g in range(2):
            low_send[2 * f + g] = landed[f * rows + rows - 2 + g]
            high_send[2 * f + g] = landed[f * rows + g]
    up = remote(low_send, low_land, rad_send.at[1], rad_recv.at[1], (az, rad_peer(1)))
    down = remote(
        high_send, high_land, rad_send.at[2], rad_recv.at[2], (az, rad_peer(rad_count - 1))
    )
    up.start()
    down.start()
    for copy in sends + returns:
        copy.wait_send()
    for copy in peak_copies:
        copy.wait_send()
    for copy in peak_copies[az_count - 1 :]:
        copy.wait_recv()
    up.wait()
    down.wait()
    low[...] = jnp.where(lowest, ghosts[...], low_land[...])
    high[...] = jnp.where(highest, ghosts[...], high_land[...])


def exchanged(fields, offsets, boundary_shift):
    parts, rows, cells, depth = fields.shape
    az_count = lax.axis_size("az")
    rad_count = lax.axis_size("rad")
    width = cells + 4
    main = parts * rows // az_count
    spare = 2 * parts // az_count
    ring_cells = cells * az_count + width + 4
    vmem = pl.BlockSpec(memory_space=pltpu.VMEM)
    smem = pl.BlockSpec(memory_space=pltpu.SMEM)

    def buffer(*shape):
        return pltpu.VMEM((*shape, depth), jnp.float32)

    edge = jax.ShapeDtypeStruct((2 * parts, width, depth), jnp.float32)
    landed, low, high, peaks = pl.pallas_call(
        functools.partial(exchange_kernel, rows, az_count, rad_count),
        out_shape=[
            jax.ShapeDtypeStruct((parts * rows, width, depth), jnp.float32),
            edge,
            edge,
            jax.ShapeDtypeStruct((rad_count, 8, depth), jnp.float32),
        ],
        in_specs=[vmem, smem, smem],
        out_specs=[vmem] * 4,
        scratch_shapes=[
            buffer(2 * parts, width),
            buffer(az_count, main + spare, width),
            buffer(2 * parts, cells),
            buffer(2 * parts, cells),
            buffer(2 * parts, width),
            buffer(2 * parts, width),
            buffer(2 * parts, width),
            buffer(2 * parts, width),
            buffer(az_count, 8),
        ]
        + [buffer(main // CHUNKS, ring_cells)] * CHUNKS
        + [buffer(spare, ring_cells)]
        + [pltpu.SemaphoreType.DMA((CHUNKS + 1, az_count))] * 4
        + [pltpu.SemaphoreType.DMA((3,))] * 2
        + [pltpu.SemaphoreType.DMA((az_count + rad_count,))] * 2,
        compiler_params=pltpu.CompilerParams(
            collective_id=0, has_side_effects=True, vmem_limit_bytes=40 * 1024 * 1024
        ),
        name="exchange",
    )(fields.reshape(parts * rows, cells, depth), offsets, boundary_shift)
    return (
        landed.reshape(parts, rows, width, depth),
        low.reshape(parts, 2, width, depth),
        high.reshape(parts, 2, width, depth),
        peaks,
    )


def local(fields, offsets, boundary_shift):
    rows, cells = fields.shape[1:3]
    landed, low, high, peaks = exchanged(fields, offsets, boundary_shift)
    return advanced(landed, low, high, peaks, rows, cells)


def solution(mesh):
    in_specs = (P(None, "rad", "az", None), P(), P())
    out_specs = P(None, "rad", "az", None)
    return jax.shard_map(local, mesh=mesh, in_specs=in_specs, out_specs=out_specs, check_vma=False)
```

```python
import functools

import jax
import jax.numpy as jnp
from jax import lax
from jax.experimental import pallas as pl
from jax.experimental.pallas import tpu as pltpu
from jax.sharding import PartitionSpec as P

GAMMA_RATIO = 5.0 / 3.0
CFL_NUMBER = 0.4
OMEGA_RATE = 1.0
SHEAR_RATE = 1.5


def primitive(state):
    density = state[0]
    inverse = 1.0 / density
    speed_x = state[1] * inverse
    speed_y = state[2] * inverse
    speed_z = state[3] * inverse
    kinetic = 0.5 * density * (speed_x * speed_x + speed_y * speed_y + speed_z * speed_z)
    magnetic = 0.5 * (state[5] * state[5] + state[6] * state[6] + state[7] * state[7])
    pressure = (GAMMA_RATIO - 1.0) * (state[4] - kinetic - magnetic)
    return (density, speed_x, speed_y, speed_z, pressure, state[5], state[6], state[7])


def fast_speed(density, pressure, normal_field, field_sq):
    sound = (GAMMA_RATIO * pressure + field_sq) / density
    spread = jnp.maximum(
        sound * sound
        - 4.0 * GAMMA_RATIO * pressure * normal_field * normal_field / (density * density),
        0.0,
    )
    return jnp.sqrt(0.5 * (sound + jnp.sqrt(spread)))


def cell_speed(primitives):
    field_sq = (
        primitives[5] * primitives[5]
        + primitives[6] * primitives[6]
        + primitives[7] * primitives[7]
    )
    total = jnp.abs(primitives[1]) + fast_speed(
        primitives[0], primitives[4], primitives[5], field_sq
    )
    total = (
        total
        + jnp.abs(primitives[2])
        + fast_speed(primitives[0], primitives[4], primitives[6], field_sq)
    )
    total = (
        total
        + jnp.abs(primitives[3])
        + fast_speed(primitives[0], primitives[4], primitives[7], field_sq)
    )
    return total


ADIABATIC = 1.0 / (GAMMA_RATIO - 1.0)
ORDERS = ((1, 2, 3), (2, 3, 1), (3, 1, 2))
MARGIN = 8


def inverse_of(values):
    return 1.0 / values


def half_slope(first_diff, second_diff):
    return 0.5 * (
        jnp.maximum(jnp.minimum(first_diff, second_diff), 0.0)
        + jnp.minimum(jnp.maximum(first_diff, second_diff), 0.0)
    )


def half_square_speed(density, pressure, normal_sq, field_sq):
    inverse = inverse_of(density)
    sound = (GAMMA_RATIO * pressure + field_sq) * inverse
    spread = sound * sound - (4.0 * GAMMA_RATIO) * pressure * normal_sq * (inverse * inverse)
    return 0.5 * (sound + jnp.sqrt(jnp.maximum(spread, 0.0)))


def star_part(values, mass, gap, outer, middle, bn, bn_sq):
    distance = outer - middle
    inverse = inverse_of(distance)
    density = mass * inverse
    product = mass * distance
    divisor = inverse_of(jnp.maximum(product - bn_sq, 0.5 * product))
    turn = bn * (middle - values[1]) * divisor
    factor = (mass * gap - bn_sq) * divisor
    root_inverse = lax.rsqrt(density)
    return (
        density,
        values[2] - values[6] * turn,
        values[3] - values[7] * turn,
        values[6] * factor,
        values[7] * factor,
        inverse,
        density * root_inverse,
        root_inverse,
    )


def face_flux(left, right):
    bn = 0.5 * (left[5] + right[5])
    bn_sq = bn * bn
    sq_left = bn_sq + left[6] * left[6] + left[7] * left[7]
    sq_right = bn_sq + right[6] * right[6] + right[7] * right[7]
    fastest = jnp.sqrt(
        jnp.maximum(
            half_square_speed(left[0], left[4], bn_sq, sq_left),
            half_square_speed(right[0], right[4], bn_sq, sq_right),
        )
    )
    lower = jnp.minimum(left[1], right[1]) - fastest
    upper = jnp.maximum(left[1], right[1]) + fastest
    gap_left = lower - left[1]
    gap_right = upper - right[1]
    mass_left = left[0] * gap_left
    mass_right = right[0] * gap_right
    press_left = left[4] + 0.5 * sq_left
    press_right = right[4] + 0.5 * sq_right
    guess = (
        mass_right * right[1] - mass_left * left[1] - press_right + press_left
    ) * inverse_of(mass_right - mass_left)
    margin = 0.1 * (upper - lower)
    middle = jnp.minimum(jnp.maximum(guess, lower + margin), upper - margin)
    star_press = press_left + mass_left * (middle - left[1])
    star_left = star_part(left, mass_left, gap_left, lower, middle, bn, bn_sq)
    star_right = star_part(right, mass_right, gap_right, upper, middle, bn, bn_sq)
    sign = jnp.where(bn > 0.0, 1.0, jnp.where(bn < 0.0, -1.0, 0.0))
    root_left, root_right = star_left[6], star_right[6]
    share = inverse_of(root_left + root_right)
    share_left = root_left * share
    share_right = root_right * share
    kick = sign * share
    cross = root_left * share_right * sign
    v_double = (
        share_left * star_left[1]
        + share_right * star_right[1]
        + (star_right[3] - star_left[3]) * kick
    )
    w_double = (
        share_left * star_left[2]
        + share_right * star_right[2]
        + (star_right[4] - star_left[4]) * kick
    )
    bt_double = (
        share_left * star_right[3]
        + share_right * star_left[3]
        + (star_right[1] - star_left[1]) * cross
    )
    bw_double = (
        share_left * star_right[4]
        + share_right * star_left[4]
        + (star_right[2] - star_left[2]) * cross
    )
    on_left = middle > 0.0

    def pick(first, second):
        return jnp.where(on_left, first, second)

    rho, u, v, w, p, bt, bw = (pick(left[c], right[c]) for c in (0, 1, 2, 3, 4, 6, 7))
    pt = pick(press_left, press_right)
    outer = pick(lower, upper)
    gap = pick(gap_left, gap_right)
    rho_s, v_s, w_s, bt_s, bw_s, inv_s, root_s, root_inv = (
        pick(a, b) for a, b in zip(star_left, star_right)
    )
    energy = (ADIABATIC - 1.0) * p + pt + 0.5 * rho * (u * u + v * v + w * w)
    work = u * bn + v * bt + w * bw
    middle_work = middle * bn
    work_s = middle_work + v_s * bt_s + w_s * bw_s
    work_d = middle_work + v_double * bt_double + w_double * bw_double
    energy_s = (gap * energy - pt * u + star_press * middle + bn * (work - work_s)) * inv_s
    side = pick(sign, -sign)
    energy_step = side * root_s * (work_d - work_s)
    alfven = jnp.abs(bn) * root_inv
    inner = middle - pick(alfven, -alfven)
    outer_on = outer > 0.0
    inner_on = inner > 0.0
    first = jnp.where(
        on_left, jnp.where(outer_on, 0.0, outer), jnp.where(inner_on | outer_on, outer, 0.0)
    )
    second = jnp.where(
        on_left, jnp.where(outer_on | inner_on, 0.0, inner), jnp.where(inner_on, inner, 0.0)
    )
    momentum = rho * u
    second_mass = second * rho_s
    return (
        momentum + first * (rho_s - rho),
        momentum * u + pt - bn_sq + first * (rho_s * middle - momentum),
        momentum * v - bn * bt + first * (rho_s * v_s - rho * v) + second_mass * (v_double - v_s),
        momentum * w - bn * bw + first * (rho_s * w_s - rho * w) + second_mass * (w_double - w_s),
        (energy + pt) * u - bn * work + first * (energy_s - energy) + second * energy_step,
        bt * u - bn * v + first * (bt_s - bt) + second * (bt_double - bt_s),
        bw * u - bn * w + first * (bw_s - bw) + second * (bw_double - bw_s),
    )


def targets(order):
    return (0, order[0], order[1], order[2], 4, order[1] + 4, order[2] + 4)


def sources(order):
    return (0, order[0], order[1], order[2], 4, order[0] + 4, order[1] + 4, order[2] + 4)


def faces_between(before, here, after, beyond):
    middle_diff = after - here
    return (
        here + half_slope(here - before, middle_diff),
        after - half_slope(middle_diff, beyond - after),
    )


def flux_between(read, order):
    pairs = [faces_between(*read(c)) for c in sources(order)]
    return face_flux([pair[0] for pair in pairs], [pair[1] for pair in pairs])


def flux_kernel(landed, low, high, peaks, out, prims, radial_flux, ring_flux):
    rows, cells = out.shape[1], out.shape[2]
    depth = out.shape[3]
    chunks = cells // 8
    width = cells + 4
    dt = CFL_NUMBER / jnp.max(peaks[...])

    def fill(i, _):
        values = primitive([landed[pl.ds((f * rows + i) * width, width)] for f in range(8)])
        for f in range(8):
            prims[f, i + 2, MARGIN - 2 : MARGIN + cells + 2] = values[f]
        return 0

    lax.fori_loop(0, rows, fill, 0)
    for g in range(2):
        for ref, row in ((low, g), (high, rows + 2 + g)):
            values = primitive([ref[f, g] for f in range(8)])
            for f in range(8):
                prims[f, row, MARGIN - 2 : MARGIN + cells + 2] = values[f]

    def radial(row, q):
        columns = slice(MARGIN + 8 * q, MARGIN + 8 * q + 8)
        return flux_between(
            lambda c: [prims[c, row + near, columns] for near in (-1, 0, 1, 2)], ORDERS[0]
        )

    for q in range(chunks):
        for c, value in enumerate(radial(1, q)):
            radial_flux[c, 8 * q : 8 * q + 8] = value

    def advance_row(i, _):
        row = i + 2
        for q in range(chunks + 1):
            begin = MARGIN - 1 + 8 * q
            fluxes = flux_between(
                lambda c: [
                    prims[c, row, begin + near : begin + near + 8] for near in (-1, 0, 1, 2)
                ],
                ORDERS[1],
            )
            for c, value in enumerate(fluxes):
                ring_flux[c, 8 * q : 8 * q + 8] = value
        for q in range(chunks):
            inside = slice(8 * q, 8 * q + 8)
            columns = slice(MARGIN + 8 * q, MARGIN + 8 * q + 8)
            change = [None] * 8

            def gather(order, values):
                for c, value in zip(targets(order), values):
                    change[c] = value if change[c] is None else change[c] + value

            upper = radial(row, q)
            gather(ORDERS[0], [value - radial_flux[c, inside] for c, value in enumerate(upper)])
            for c, value in enumerate(upper):
                radial_flux[c, inside] = value
            gather(
                ORDERS[1],
                [ring_flux[c, 8 * q + 1 : 8 * q + 9] - ring_flux[c, inside] for c in range(7)],
            )
            lefts, rights = [], []
            for c in sources(ORDERS[2]):
                here = prims[c, row, columns]
                diff = pltpu.roll(here, depth - 1, 1) - here
                slope = half_slope(pltpu.roll(diff, 1, 1), diff)
                lefts.append(here + slope)
                rights.append(pltpu.roll(here - slope, depth - 1, 1))
            above = face_flux(lefts, rights)
            gather(ORDERS[2], [value - pltpu.roll(value, 1, 1) for value in above])
            state = [landed[pl.ds((f * rows + i) * width + 8 * q + 2, 8)] for f in range(8)]
            speed_x = prims[1, row, columns]
            gains = {
                1: (2.0 * OMEGA_RATE) * state[2],
                2: (-(2.0 - SHEAR_RATE) * OMEGA_RATE) * state[1],
                4: (SHEAR_RATE * OMEGA_RATE) * (speed_x * state[2] - state[5] * state[6]),
                6: (-SHEAR_RATE * OMEGA_RATE) * state[5],
            }
            for f in range(8):
                total = gains[f] - change[f] if f in gains else -change[f]
                out[f, i, inside] = state[f] + dt * total
        return 0

    lax.fori_loop(0, rows, advance_row, 0)


def advanced(landed, low, high, peaks, rows, cells):
    parts, depth = low.shape[0], low.shape[3]
    vmem = pl.BlockSpec(memory_space=pltpu.VMEM)
    return pl.pallas_call(
        flux_kernel,
        out_shape=jax.ShapeDtypeStruct((parts, rows, cells, depth), jnp.float32),
        in_specs=[vmem] * 4,
        out_specs=vmem,
        scratch_shapes=[
            pltpu.VMEM((parts, rows + 4, cells + 3 * MARGIN, depth), jnp.float32),
            pltpu.VMEM((7, cells, depth), jnp.float32),
            pltpu.VMEM((7, cells + 8, depth), jnp.float32),
        ],
        compiler_params=pltpu.CompilerParams(vmem_limit_bytes=40 * 1024 * 1024),
        name="advance",
    )(landed, low, high, peaks)


CHUNKS = 4


def exchange_kernel(
    rows, az_count, rad_count,
    fields, offsets, shear,
    landed, low, high, rad_peaks,
    ghosts, windows, ghost_windows, ghost_send, ghost_land, low_send, high_send, low_land, high_land, az_peaks,
    *rest,
):
    rings = rest[: CHUNKS + 1]
    out_send, out_recv, back_send, back_recv, rad_send, rad_recv, peak_send, peak_recv = rest[
        CHUNKS + 1 : CHUNKS + 9
    ]
    barrier = pltpu.get_barrier_semaphore()
    az = lax.axis_index("az")
    rad = lax.axis_index("rad")
    cells = fields.shape[1]
    width = low.shape[1]
    loop_cells = cells * az_count
    radial_cells = rows * rad_count
    parts = fields.shape[0] // rows
    spare = 2 * parts // az_count
    band = rows // CHUNKS
    piece = parts * band // az_count
    peers = sorted(range(1, az_count), key=lambda k: -min(k, az_count - k))
    order = [0, CHUNKS - 1, CHUNKS, *range(1, CHUNKS - 1)]
    lowest = rad == 0
    highest = rad == rad_count - 1

    def az_peer(k):
        return lax.rem(az + k, az_count)

    def rad_peer(k):
        return lax.rem(rad + k, rad_count)

    for k in range(1, az_count):
        pl.semaphore_signal(
            barrier, inc=1, device_id=(az_peer(k), rad), device_id_type=pl.DeviceIdType.MESH
        )
    for k in range(1, rad_count):
        pl.semaphore_signal(
            barrier, inc=1, device_id=(az, rad_peer(k)), device_id_type=pl.DeviceIdType.MESH
        )
    pl.semaphore_wait(barrier, az_count + rad_count - 2)

    def remote(src, dst, send, recv, target):
        return pltpu.make_async_remote_copy(
            src_ref=src,
            dst_ref=dst,
            send_sem=send,
            recv_sem=recv,
            device_id=target,
            device_id_type=pl.DeviceIdType.MESH,
        )

    def unit(device, c):
        flat = device * piece
        return lax.div(flat, band) * rows + c * band + lax.rem(flat, band)

    def packed(start, count):
        return pl.ds(pl.multiple_of(start * width, 8), count * width)

    for f in range(parts):
        for g in range(2):
            edge = jnp.where(lowest, g, rows - 2 + g)
            ghost_send[2 * f + g] = fields[f * rows + edge]
    ghost_copy = remote(
        ghost_send, ghost_land, rad_send.at[0], rad_recv.at[0], (az, rad_count - 1 - rad)
    )
    ghost_copy.start()

    own = pl.ds(pl.multiple_of(az * cells, cells), cells)

    def outward(c, k):
        peer = az_peer(k)
        if c < CHUNKS:
            src = fields.at[pl.ds(unit(peer, c), piece)]
        else:
            src = ghost_land.at[pl.ds(peer * spare, spare)]
        return remote(
            src, rings[c].at[:, own], out_send.at[c, k], out_recv.at[c, k], (peer, rad)
        )

    sends = []
    for c in order:
        if c == CHUNKS:
            ghost_copy.wait()
            rings[c][:, own] = ghost_land[pl.ds(az * spare, spare)]
        else:
            rings[c][:, own] = fields[pl.ds(unit(az, c), piece)]
        for k in peers:
            sends.append(outward(c, k))
            sends[-1].start()

    def peak_of(i, best):
        return jnp.maximum(
            best, cell_speed(primitive([fields[f * rows + i] for f in range(parts)]))
        )

    best = lax.fori_loop(0, rows, peak_of, jnp.zeros(fields.shape[1:], jnp.float32))
    tile = best[:8]
    for q in range(1, cells // 8):
        tile = jnp.maximum(tile, best[8 * q : 8 * q + 8])
    az_peaks[az] = tile
    peak_copies = []
    for k in range(1, az_count):
        peak_copies.append(
            remote(
                az_peaks.at[az],
                az_peaks.at[az],
                peak_send.at[k],
                peak_recv.at[k],
                (az_peer(k), rad),
            )
        )
        peak_copies[-1].start()

    returns = []

    def backward(c, k):
        peer = az_peer(k)
        if c < CHUNKS:
            source = windows.at[peer, c * piece * width : (c + 1) * piece * width]
            place = landed.at[packed(unit(az, c), piece)]
        else:
            source = ghost_windows.at[peer]
            place = ghosts.at[pl.ds(az * spare, spare)]
        return remote(source, place, back_send.at[c, k], back_recv.at[c, k], (peer, rad))

    def edges_out(c, source, send, land, slot, step):
        begin = 0 if c == 0 else rows - 2
        for f in range(parts):
            for g in range(2):
                at = (f * rows + begin + g) * width
                send[2 * f + g] = source[at : at + width]
        copy = remote(send, land, rad_send.at[slot], rad_recv.at[slot], (az, rad_peer(step)))
        copy.start()
        return copy

    def collect(c):
        for copy, chunk in returns:
            if chunk == c:
                copy.wait_recv()

    for c in order:
        for k in peers:
            outward(c, k).wait_recv()
        count = piece if c < CHUNKS else spare
        ring = rings[c]
        for u in range(count):
            ring[u, loop_cells : loop_cells + width + 4] = ring[u, : width + 4]
        for u in range(count):
            if c < CHUNKS:
                row = rad * rows + lax.rem(unit(az, c), rows) + u
                shift = offsets[row]
            else:
                g = lax.rem(az * spare + u, 2)
                row = jnp.where(lowest, radial_cells - 2, 0) + g
                shift = offsets[row] + jnp.where(lowest, shear[0], -shear[0])
            for t in range(az_count):
                start = lax.rem(t * cells - 2 - shift + 4 * loop_cells, loop_cells)
                window = ring[u, pl.ds(start, width)]
                if c < CHUNKS:
                    at = (c * piece + u) * width
                    windows[t, at : at + width] = window
                else:
                    ghost_windows[t, u] = window
        for k in peers:
            copy = backward(c, k)
            copy.start()
            returns.append((copy, c))
        if c < CHUNKS:
            landed[packed(unit(az, c), piece)] = windows[
                az, c * piece * width : (c + 1) * piece * width
            ]
        else:
            ghosts[pl.ds(az * spare, spare)] = ghost_windows[az]

    for copy in peak_copies:
        copy.wait_recv()
    tile = az_peaks[0]
    for a in range(1, az_count):
        tile = jnp.maximum(tile, az_peaks[a])
    rad_peaks[rad] = tile
    for k in range(1, rad_count):
        copy = remote(
            rad_peaks.at[rad],
            rad_peaks.at[rad],
            peak_send.at[az_count + k],
            peak_recv.at[az_count + k],
            (az, rad_peer(k)),
        )
        peak_copies.append(copy)
        copy.start()

    collect(0)
    down = edges_out(0, landed, high_send, high_land, 2, rad_count - 1)
    collect(CHUNKS - 1)
    up = edges_out(CHUNKS - 1, landed, low_send, low_land, 1, 1)
    collect(CHUNKS)
    for copy in peak_copies[az_count - 1 :]:
        copy.wait_recv()
    for copy in sends + peak_copies:
        copy.wait_send()
    up.wait()
    down.wait()
    low[...] = jnp.where(lowest, ghosts[...], low_land[...])
    high[...] = jnp.where(highest, ghosts[...], high_land[...])
    for c in range(1, CHUNKS - 1):
        collect(c)
    for copy, _ in returns:
        copy.wait_send()


def exchanged(fields, offsets, boundary_shift):
    parts, rows, cells, depth = fields.shape
    az_count = lax.axis_size("az")
    rad_count = lax.axis_size("rad")
    width = cells + 4
    piece = parts * rows // CHUNKS // az_count
    spare = 2 * parts // az_count
    ring_cells = cells * az_count + width + 4
    vmem = pl.BlockSpec(memory_space=pltpu.VMEM)
    smem = pl.BlockSpec(memory_space=pltpu.SMEM)

    def buffer(*shape):
        return pltpu.VMEM((*shape, depth), jnp.float32)

    edge = jax.ShapeDtypeStruct((2 * parts, width, depth), jnp.float32)
    landed, low, high, peaks = pl.pallas_call(
        functools.partial(exchange_kernel, rows, az_count, rad_count),
        out_shape=[
            jax.ShapeDtypeStruct((parts * rows * width, depth), jnp.float32),
            edge,
            edge,
            jax.ShapeDtypeStruct((rad_count, 8, depth), jnp.float32),
        ],
        in_specs=[vmem, smem, smem],
        out_specs=[vmem] * 4,
        scratch_shapes=[
            buffer(2 * parts, width),
            buffer(az_count, CHUNKS * piece * width),
            buffer(az_count, spare, width),
            buffer(2 * parts, cells),
            buffer(2 * parts, cells),
            buffer(2 * parts, width),
            buffer(2 * parts, width),
            buffer(2 * parts, width),
            buffer(2 * parts, width),
            buffer(az_count, 8),
        ]
        + [buffer(piece, ring_cells)] * CHUNKS
        + [buffer(spare, ring_cells)]
        + [pltpu.SemaphoreType.DMA((CHUNKS + 1, az_count))] * 4
        + [pltpu.SemaphoreType.DMA((3,))] * 2
        + [pltpu.SemaphoreType.DMA((az_count + rad_count,))] * 2,
        compiler_params=pltpu.CompilerParams(
            collective_id=0, has_side_effects=True, vmem_limit_bytes=40 * 1024 * 1024
        ),
        name="exchange",
    )(fields.reshape(parts * rows, cells, depth), offsets, boundary_shift)
    return (
        landed,
        low.reshape(parts, 2, width, depth),
        high.reshape(parts, 2, width, depth),
        peaks,
    )


def local(fields, offsets, boundary_shift):
    rows, cells = fields.shape[1:3]
    landed, low, high, peaks = exchanged(fields, offsets, boundary_shift)
    return advanced(landed, low, high, peaks, rows, cells)


def solution(mesh):
    in_specs = (P(None, "rad", "az", None), P(), P())
    out_specs = P(None, "rad", "az", None)
    return jax.shard_map(local, mesh=mesh, in_specs=in_specs, out_specs=out_specs, check_vma=False)
```

```python
import functools

import jax
import jax.numpy as jnp
from jax import lax
from jax.experimental import pallas as pl
from jax.experimental.pallas import tpu as pltpu
from jax.sharding import PartitionSpec as P

GAMMA_RATIO = 5.0 / 3.0
CFL_NUMBER = 0.4
OMEGA_RATE = 1.0
SHEAR_RATE = 1.5


def primitive(state):
    density = state[0]
    inverse = 1.0 / density
    speed_x = state[1] * inverse
    speed_y = state[2] * inverse
    speed_z = state[3] * inverse
    kinetic = 0.5 * density * (speed_x * speed_x + speed_y * speed_y + speed_z * speed_z)
    magnetic = 0.5 * (state[5] * state[5] + state[6] * state[6] + state[7] * state[7])
    pressure = (GAMMA_RATIO - 1.0) * (state[4] - kinetic - magnetic)
    return (density, speed_x, speed_y, speed_z, pressure, state[5], state[6], state[7])


def fast_speed(density, pressure, normal_field, field_sq):
    sound = (GAMMA_RATIO * pressure + field_sq) / density
    spread = jnp.maximum(
        sound * sound
        - 4.0 * GAMMA_RATIO * pressure * normal_field * normal_field / (density * density),
        0.0,
    )
    return jnp.sqrt(0.5 * (sound + jnp.sqrt(spread)))


def cell_speed(primitives):
    field_sq = (
        primitives[5] * primitives[5]
        + primitives[6] * primitives[6]
        + primitives[7] * primitives[7]
    )
    total = jnp.abs(primitives[1]) + fast_speed(
        primitives[0], primitives[4], primitives[5], field_sq
    )
    total = (
        total
        + jnp.abs(primitives[2])
        + fast_speed(primitives[0], primitives[4], primitives[6], field_sq)
    )
    total = (
        total
        + jnp.abs(primitives[3])
        + fast_speed(primitives[0], primitives[4], primitives[7], field_sq)
    )
    return total


ADIABATIC = 1.0 / (GAMMA_RATIO - 1.0)
ORDERS = ((1, 2, 3), (2, 3, 1), (3, 1, 2))
MARGIN = 8


def inverse_of(values):
    return 1.0 / values


def half_slope(first_diff, second_diff):
    return 0.5 * (
        jnp.maximum(jnp.minimum(first_diff, second_diff), 0.0)
        + jnp.minimum(jnp.maximum(first_diff, second_diff), 0.0)
    )


def half_square_speed(density, pressure, normal_sq, field_sq):
    inverse = inverse_of(density)
    sound = (GAMMA_RATIO * pressure + field_sq) * inverse
    spread = sound * sound - (4.0 * GAMMA_RATIO) * pressure * normal_sq * (inverse * inverse)
    return 0.5 * (sound + jnp.sqrt(jnp.maximum(spread, 0.0)))


def star_part(values, mass, gap, outer, middle, bn, bn_sq):
    distance = outer - middle
    inverse = inverse_of(distance)
    density = mass * inverse
    product = mass * distance
    divisor = inverse_of(jnp.maximum(product - bn_sq, 0.5 * product))
    turn = bn * (middle - values[1]) * divisor
    factor = (mass * gap - bn_sq) * divisor
    root_inverse = lax.rsqrt(density)
    return (
        density,
        values[2] - values[6] * turn,
        values[3] - values[7] * turn,
        values[6] * factor,
        values[7] * factor,
        inverse,
        density * root_inverse,
        root_inverse,
    )


def face_flux(left, right):
    bn = 0.5 * (left[5] + right[5])
    bn_sq = bn * bn
    sq_left = bn_sq + left[6] * left[6] + left[7] * left[7]
    sq_right = bn_sq + right[6] * right[6] + right[7] * right[7]
    fastest = jnp.sqrt(
        jnp.maximum(
            half_square_speed(left[0], left[4], bn_sq, sq_left),
            half_square_speed(right[0], right[4], bn_sq, sq_right),
        )
    )
    lower = jnp.minimum(left[1], right[1]) - fastest
    upper = jnp.maximum(left[1], right[1]) + fastest
    gap_left = lower - left[1]
    gap_right = upper - right[1]
    mass_left = left[0] * gap_left
    mass_right = right[0] * gap_right
    press_left = left[4] + 0.5 * sq_left
    press_right = right[4] + 0.5 * sq_right
    guess = (
        mass_right * right[1] - mass_left * left[1] - press_right + press_left
    ) * inverse_of(mass_right - mass_left)
    margin = 0.1 * (upper - lower)
    middle = jnp.minimum(jnp.maximum(guess, lower + margin), upper - margin)
    star_press = press_left + mass_left * (middle - left[1])
    star_left = star_part(left, mass_left, gap_left, lower, middle, bn, bn_sq)
    star_right = star_part(right, mass_right, gap_right, upper, middle, bn, bn_sq)
    sign = jnp.where(bn > 0.0, 1.0, jnp.where(bn < 0.0, -1.0, 0.0))
    root_left, root_right = star_left[6], star_right[6]
    share = inverse_of(root_left + root_right)
    share_left = root_left * share
    share_right = root_right * share
    kick = sign * share
    cross = root_left * share_right * sign
    v_double = (
        share_left * star_left[1]
        + share_right * star_right[1]
        + (star_right[3] - star_left[3]) * kick
    )
    w_double = (
        share_left * star_left[2]
        + share_right * star_right[2]
        + (star_right[4] - star_left[4]) * kick
    )
    bt_double = (
        share_left * star_right[3]
        + share_right * star_left[3]
        + (star_right[1] - star_left[1]) * cross
    )
    bw_double = (
        share_left * star_right[4]
        + share_right * star_left[4]
        + (star_right[2] - star_left[2]) * cross
    )
    on_left = middle > 0.0

    def pick(first, second):
        return jnp.where(on_left, first, second)

    rho, u, v, w, p, bt, bw = (pick(left[c], right[c]) for c in (0, 1, 2, 3, 4, 6, 7))
    pt = pick(press_left, press_right)
    outer = pick(lower, upper)
    gap = pick(gap_left, gap_right)
    rho_s, v_s, w_s, bt_s, bw_s, inv_s, root_s, root_inv = (
        pick(a, b) for a, b in zip(star_left, star_right)
    )
    energy = (ADIABATIC - 1.0) * p + pt + 0.5 * rho * (u * u + v * v + w * w)
    work = u * bn + v * bt + w * bw
    middle_work = middle * bn
    work_s = middle_work + v_s * bt_s + w_s * bw_s
    work_d = middle_work + v_double * bt_double + w_double * bw_double
    energy_s = (gap * energy - pt * u + star_press * middle + bn * (work - work_s)) * inv_s
    side = pick(sign, -sign)
    energy_step = side * root_s * (work_d - work_s)
    alfven = jnp.abs(bn) * root_inv
    inner = middle - pick(alfven, -alfven)
    outer_on = outer > 0.0
    inner_on = inner > 0.0
    first = jnp.where(
        on_left, jnp.where(outer_on, 0.0, outer), jnp.where(inner_on | outer_on, outer, 0.0)
    )
    second = jnp.where(
        on_left, jnp.where(outer_on | inner_on, 0.0, inner), jnp.where(inner_on, inner, 0.0)
    )
    momentum = rho * u
    second_mass = second * rho_s
    return (
        momentum + first * (rho_s - rho),
        momentum * u + pt - bn_sq + first * (rho_s * middle - momentum),
        momentum * v - bn * bt + first * (rho_s * v_s - rho * v) + second_mass * (v_double - v_s),
        momentum * w - bn * bw + first * (rho_s * w_s - rho * w) + second_mass * (w_double - w_s),
        (energy + pt) * u - bn * work + first * (energy_s - energy) + second * energy_step,
        bt * u - bn * v + first * (bt_s - bt) + second * (bt_double - bt_s),
        bw * u - bn * w + first * (bw_s - bw) + second * (bw_double - bw_s),
    )


def targets(order):
    return (0, order[0], order[1], order[2], 4, order[1] + 4, order[2] + 4)


def sources(order):
    return (0, order[0], order[1], order[2], 4, order[0] + 4, order[1] + 4, order[2] + 4)


def faces_between(before, here, after, beyond):
    middle_diff = after - here
    return (
        here + half_slope(here - before, middle_diff),
        after - half_slope(middle_diff, beyond - after),
    )


def flux_between(read, order):
    pairs = [faces_between(*read(c)) for c in sources(order)]
    return face_flux([pair[0] for pair in pairs], [pair[1] for pair in pairs])


def flux_kernel(landed, low, high, peaks, out, prims, radial_flux, ring_flux):
    rows, cells = out.shape[1], out.shape[2]
    depth = out.shape[3]
    chunks = cells // 8
    width = cells + 4
    dt = CFL_NUMBER / jnp.max(peaks[...])

    def fill(i, _):
        values = primitive([landed[pl.ds((f * rows + i) * width, width)] for f in range(8)])
        for f in range(8):
            prims[f, i + 2, MARGIN - 2 : MARGIN + cells + 2] = values[f]
        return 0

    lax.fori_loop(0, rows, fill, 0)
    for g in range(2):
        for ref, row in ((low, g), (high, rows + 2 + g)):
            values = primitive([ref[f, g] for f in range(8)])
            for f in range(8):
                prims[f, row, MARGIN - 2 : MARGIN + cells + 2] = values[f]

    def radial(row, q):
        columns = slice(MARGIN + 8 * q, MARGIN + 8 * q + 8)
        return flux_between(
            lambda c: [prims[c, row + near, columns] for near in (-1, 0, 1, 2)], ORDERS[0]
        )

    for q in range(chunks):
        for c, value in enumerate(radial(1, q)):
            radial_flux[c, 8 * q : 8 * q + 8] = value

    def advance_row(i, _):
        row = i + 2
        for q in range(chunks + 1):
            begin = MARGIN - 1 + 8 * q
            fluxes = flux_between(
                lambda c: [
                    prims[c, row, begin + near : begin + near + 8] for near in (-1, 0, 1, 2)
                ],
                ORDERS[1],
            )
            for c, value in enumerate(fluxes):
                ring_flux[c, 8 * q : 8 * q + 8] = value
        for q in range(chunks):
            inside = slice(8 * q, 8 * q + 8)
            columns = slice(MARGIN + 8 * q, MARGIN + 8 * q + 8)
            change = [None] * 8

            def gather(order, values):
                for c, value in zip(targets(order), values):
                    change[c] = value if change[c] is None else change[c] + value

            upper = radial(row, q)
            gather(ORDERS[0], [value - radial_flux[c, inside] for c, value in enumerate(upper)])
            for c, value in enumerate(upper):
                radial_flux[c, inside] = value
            gather(
                ORDERS[1],
                [ring_flux[c, 8 * q + 1 : 8 * q + 9] - ring_flux[c, inside] for c in range(7)],
            )
            lefts, rights = [], []
            for c in sources(ORDERS[2]):
                here = prims[c, row, columns]
                diff = pltpu.roll(here, depth - 1, 1) - here
                slope = half_slope(pltpu.roll(diff, 1, 1), diff)
                lefts.append(here + slope)
                rights.append(pltpu.roll(here - slope, depth - 1, 1))
            above = face_flux(lefts, rights)
            gather(ORDERS[2], [value - pltpu.roll(value, 1, 1) for value in above])
            state = [landed[pl.ds((f * rows + i) * width + 8 * q + 2, 8)] for f in range(8)]
            speed_x = prims[1, row, columns]
            gains = {
                1: (2.0 * OMEGA_RATE) * state[2],
                2: (-(2.0 - SHEAR_RATE) * OMEGA_RATE) * state[1],
                4: (SHEAR_RATE * OMEGA_RATE) * (speed_x * state[2] - state[5] * state[6]),
                6: (-SHEAR_RATE * OMEGA_RATE) * state[5],
            }
            for f in range(8):
                total = gains[f] - change[f] if f in gains else -change[f]
                out[f, i, inside] = state[f] + dt * total
        return 0

    lax.fori_loop(0, rows, advance_row, 0)


def advanced(landed, low, high, peaks, rows, cells):
    parts, depth = low.shape[0], low.shape[3]
    vmem = pl.BlockSpec(memory_space=pltpu.VMEM)
    return pl.pallas_call(
        flux_kernel,
        out_shape=jax.ShapeDtypeStruct((parts, rows, cells, depth), jnp.float32),
        in_specs=[vmem] * 4,
        out_specs=vmem,
        scratch_shapes=[
            pltpu.VMEM((parts, rows + 4, cells + 3 * MARGIN, depth), jnp.float32),
            pltpu.VMEM((7, cells, depth), jnp.float32),
            pltpu.VMEM((7, cells + 8, depth), jnp.float32),
        ],
        compiler_params=pltpu.CompilerParams(vmem_limit_bytes=40 * 1024 * 1024),
        name="advance",
    )(landed, low, high, peaks)


CHUNKS = 4


def exchange_kernel(
    rows, az_count, rad_count,
    fields, offsets, shear,
    landed, low, high, rad_peaks,
    ghosts, windows, ghost_windows, ghost_send, ghost_land, low_send, high_send, low_land, high_land, az_peaks,
    *rest,
):
    rings = rest[: CHUNKS + 1]
    out_send, out_recv, back_send, back_recv, rad_send, rad_recv, peak_send, peak_recv = rest[
        CHUNKS + 1 : CHUNKS + 9
    ]
    barrier = pltpu.get_barrier_semaphore()
    az = lax.axis_index("az")
    rad = lax.axis_index("rad")
    cells = fields.shape[1]
    width = low.shape[1]
    loop_cells = cells * az_count
    radial_cells = rows * rad_count
    parts = fields.shape[0] // rows
    spare = 2 * parts // az_count
    band = rows // CHUNKS
    piece = parts * band // az_count
    peers = sorted(range(1, az_count), key=lambda k: -min(k, az_count - k))
    order = [0, CHUNKS - 1, *range(1, CHUNKS - 1), CHUNKS]
    lowest = rad == 0
    highest = rad == rad_count - 1

    def az_peer(k):
        return lax.rem(az + k, az_count)

    def rad_peer(k):
        return lax.rem(rad + k, rad_count)

    for k in range(1, az_count):
        pl.semaphore_signal(
            barrier, inc=1, device_id=(az_peer(k), rad), device_id_type=pl.DeviceIdType.MESH
        )
    for k in range(1, rad_count):
        pl.semaphore_signal(
            barrier, inc=1, device_id=(az, rad_peer(k)), device_id_type=pl.DeviceIdType.MESH
        )
    pl.semaphore_wait(barrier, az_count + rad_count - 2)

    def remote(src, dst, send, recv, target):
        return pltpu.make_async_remote_copy(
            src_ref=src,
            dst_ref=dst,
            send_sem=send,
            recv_sem=recv,
            device_id=target,
            device_id_type=pl.DeviceIdType.MESH,
        )

    def unit(device, c):
        flat = device * piece
        return lax.div(flat, band) * rows + c * band + lax.rem(flat, band)

    def packed(start, count):
        return pl.ds(pl.multiple_of(start * width, 8), count * width)

    for f in range(parts):
        for g in range(2):
            edge = jnp.where(lowest, g, rows - 2 + g)
            ghost_send[2 * f + g] = fields[f * rows + edge]
    ghost_copy = remote(
        ghost_send, ghost_land, rad_send.at[0], rad_recv.at[0], (az, rad_count - 1 - rad)
    )
    ghost_copy.start()

    own = pl.ds(pl.multiple_of(az * cells, cells), cells)

    def outward(c, k):
        peer = az_peer(k)
        if c < CHUNKS:
            src = fields.at[pl.ds(unit(peer, c), piece)]
        else:
            src = ghost_land.at[pl.ds(peer * spare, spare)]
        return remote(
            src, rings[c].at[:, own], out_send.at[c, k], out_recv.at[c, k], (peer, rad)
        )

    sends = []
    for c in order:
        if c == CHUNKS:
            ghost_copy.wait()
            rings[c][:, own] = ghost_land[pl.ds(az * spare, spare)]
        else:
            rings[c][:, own] = fields[pl.ds(unit(az, c), piece)]
        for k in peers:
            sends.append(outward(c, k))
            sends[-1].start()

    def peak_of(i, best):
        return jnp.maximum(
            best, cell_speed(primitive([fields[f * rows + i] for f in range(parts)]))
        )

    best = lax.fori_loop(0, rows, peak_of, jnp.zeros(fields.shape[1:], jnp.float32))
    tile = best[:8]
    for q in range(1, cells // 8):
        tile = jnp.maximum(tile, best[8 * q : 8 * q + 8])
    az_peaks[az] = tile
    peak_copies = []
    for k in range(1, az_count):
        peak_copies.append(
            remote(
                az_peaks.at[az],
                az_peaks.at[az],
                peak_send.at[k],
                peak_recv.at[k],
                (az_peer(k), rad),
            )
        )
        peak_copies[-1].start()

    returns = []

    def backward(c, k):
        peer = az_peer(k)
        if c < CHUNKS:
            source = windows.at[peer, c * piece * width : (c + 1) * piece * width]
            place = landed.at[packed(unit(az, c), piece)]
        else:
            source = ghost_windows.at[peer]
            place = ghosts.at[pl.ds(az * spare, spare)]
        return remote(source, place, back_send.at[c, k], back_recv.at[c, k], (peer, rad))

    def edges_out(c, source, send, land, slot, step):
        begin = 0 if c == 0 else rows - 2
        for f in range(parts):
            for g in range(2):
                at = (f * rows + begin + g) * width
                send[2 * f + g] = source[at : at + width]
        copy = remote(send, land, rad_send.at[slot], rad_recv.at[slot], (az, rad_peer(step)))
        copy.start()
        return copy

    def collect(c):
        for copy, chunk in returns:
            if chunk == c:
                copy.wait_recv()

    for c in order:
        for k in peers:
            outward(c, k).wait_recv()
        count = piece if c < CHUNKS else spare
        ring = rings[c]
        for u in range(count):
            ring[u, loop_cells : loop_cells + width + 4] = ring[u, : width + 4]
        for u in range(count):
            if c < CHUNKS:
                row = rad * rows + lax.rem(unit(az, c), rows) + u
                shift = offsets[row]
            else:
                g = lax.rem(az * spare + u, 2)
                row = jnp.where(lowest, radial_cells - 2, 0) + g
                shift = offsets[row] + jnp.where(lowest, shear[0], -shear[0])
            for t in range(az_count):
                start = lax.rem(t * cells - 2 - shift + 4 * loop_cells, loop_cells)
                window = ring[u, pl.ds(start, width)]
                if c < CHUNKS:
                    at = (c * piece + u) * width
                    windows[t, at : at + width] = window
                else:
                    ghost_windows[t, u] = window
        for k in peers:
            copy = backward(c, k)
            copy.start()
            returns.append((copy, c))
        if c < CHUNKS:
            landed[packed(unit(az, c), piece)] = windows[
                az, c * piece * width : (c + 1) * piece * width
            ]
        else:
            ghosts[pl.ds(az * spare, spare)] = ghost_windows[az]

    for copy in peak_copies:
        copy.wait_recv()
    tile = az_peaks[0]
    for a in range(1, az_count):
        tile = jnp.maximum(tile, az_peaks[a])
    rad_peaks[rad] = tile
    for k in range(1, rad_count):
        copy = remote(
            rad_peaks.at[rad],
            rad_peaks.at[rad],
            peak_send.at[az_count + k],
            peak_recv.at[az_count + k],
            (az, rad_peer(k)),
        )
        peak_copies.append(copy)
        copy.start()

    collect(0)
    down = edges_out(0, landed, high_send, high_land, 2, rad_count - 1)
    collect(CHUNKS - 1)
    up = edges_out(CHUNKS - 1, landed, low_send, low_land, 1, 1)
    for copy in peak_copies[az_count - 1 :]:
        copy.wait_recv()
    for copy in sends + peak_copies:
        copy.wait_send()
    up.wait()
    down.wait()
    for c in range(1, CHUNKS - 1):
        collect(c)
    collect(CHUNKS)
    low[...] = jnp.where(lowest, ghosts[...], low_land[...])
    high[...] = jnp.where(highest, ghosts[...], high_land[...])
    for copy, _ in returns:
        copy.wait_send()


def exchanged(fields, offsets, boundary_shift):
    parts, rows, cells, depth = fields.shape
    az_count = lax.axis_size("az")
    rad_count = lax.axis_size("rad")
    width = cells + 4
    piece = parts * rows // CHUNKS // az_count
    spare = 2 * parts // az_count
    ring_cells = cells * az_count + width + 4
    vmem = pl.BlockSpec(memory_space=pltpu.VMEM)
    smem = pl.BlockSpec(memory_space=pltpu.SMEM)

    def buffer(*shape):
        return pltpu.VMEM((*shape, depth), jnp.float32)

    edge = jax.ShapeDtypeStruct((2 * parts, width, depth), jnp.float32)
    landed, low, high, peaks = pl.pallas_call(
        functools.partial(exchange_kernel, rows, az_count, rad_count),
        out_shape=[
            jax.ShapeDtypeStruct((parts * rows * width, depth), jnp.float32),
            edge,
            edge,
            jax.ShapeDtypeStruct((rad_count, 8, depth), jnp.float32),
        ],
        in_specs=[vmem, smem, smem],
        out_specs=[vmem] * 4,
        scratch_shapes=[
            buffer(2 * parts, width),
            buffer(az_count, CHUNKS * piece * width),
            buffer(az_count, spare, width),
            buffer(2 * parts, cells),
            buffer(2 * parts, cells),
            buffer(2 * parts, width),
            buffer(2 * parts, width),
            buffer(2 * parts, width),
            buffer(2 * parts, width),
            buffer(az_count, 8),
        ]
        + [buffer(piece, ring_cells)] * CHUNKS
        + [buffer(spare, ring_cells)]
        + [pltpu.SemaphoreType.DMA((CHUNKS + 1, az_count))] * 4
        + [pltpu.SemaphoreType.DMA((3,))] * 2
        + [pltpu.SemaphoreType.DMA((az_count + rad_count,))] * 2,
        compiler_params=pltpu.CompilerParams(
            collective_id=0, has_side_effects=True, vmem_limit_bytes=40 * 1024 * 1024
        ),
        name="exchange",
    )(fields.reshape(parts * rows, cells, depth), offsets, boundary_shift)
    return (
        landed,
        low.reshape(parts, 2, width, depth),
        high.reshape(parts, 2, width, depth),
        peaks,
    )


def local(fields, offsets, boundary_shift):
    rows, cells = fields.shape[1:3]
    landed, low, high, peaks = exchanged(fields, offsets, boundary_shift)
    return advanced(landed, low, high, peaks, rows, cells)


def solution(mesh):
    in_specs = (P(None, "rad", "az", None), P(), P())
    out_specs = P(None, "rad", "az", None)
    return jax.shard_map(local, mesh=mesh, in_specs=in_specs, out_specs=out_specs, check_vma=False)
```
